32 devices in a mesh: inp: 8 (over y, x, core), tm: 4 (over z).
Axes of the slice: x: 2, y: 2, z: 4, core: 2. Of those that a mesh axis runs over, the one named last changes fastest.
Arguments:
- voltages: bfloat16 [1024, 262144], P('inp', 'tm'), may hold values from -6 to 6
- prototype: float32 [8, 1024], replicated, may hold values from -2 to 2
Outputs:
- correlation: bfloat16 [512, 2, 1024, 1024], P(('inp', 'tm'))
The draws below stay inside these ranges and needn't reach their ends.
All inputs are finite; a program needn't handle non-finite values.
Results may differ from the reference program's by a relative error of at most 0.0065.
Values may be sent and summed in bfloat16 or wider, within the bound.
No kernel may reach another device: no remote copies, remote signals or barrier semaphores. Data moves between devices by JAX's collectives and lax.ppermute only.
A program may use at most 192 MiB of HBM per device.

```python
import math
import jax
import jax.numpy as jnp
from jax import lax

INPUTS = 1024
CHAN = 512
TAPS = 8
FRAME = 1024
SPEC = 256
SAMPLES = 262144


def levels(key, shape, pieces, least, top_value):
    level, own = 1.0, jax.random.fold_in(key, 6)
    for axis_at, blocks in pieces:
        steps = jnp.exp(jax.random.uniform(jax.random.fold_in(own, axis_at), (blocks,), jnp.float32, least / len(pieces), top_value / len(pieces)))
        level = level * jnp.repeat(steps, shape[axis_at] // blocks).reshape([-1 if axis == axis_at else 1 for axis in range(len(shape))])
    return level


def gaussian(stream_key, extent, spread, bound, cuts=(), kind=jnp.bfloat16):
    array = jax.random.normal(stream_key, extent, jnp.float32) * spread
    if len(cuts) > 0:
        array = levels(stream_key, extent, cuts, -0.22, 0.18) * array
    return jnp.clip(array, min=-bound, max=bound).astype(kind)


def setup_inputs(seed: int = 0) -> dict:
    keys = jax.random.split(jax.random.key(seed), 3)
    voltages = gaussian(keys[0], (INPUTS, SAMPLES), 1.0, 6.0, ((0, 8), (1, 4)))
    prototype = gaussian(keys[1], (TAPS, FRAME), 0.35, 2.0, (), jnp.float32)
    return dict(voltages=voltages, prototype=prototype)


def dft_table(frame):
    sample = jnp.arange(frame, dtype=jnp.int32)[:, None]
    column = jnp.arange(frame, dtype=jnp.int32)[None, :]
    phase = (sample * (column // 2) % frame).astype(jnp.float32) * (2.0 * math.pi / frame)
    table = jnp.where(column % 2 == 0, jnp.cos(phase), -jnp.sin(phase))
    return table.astype(jnp.bfloat16)

def channelize(frames, earlier, prototype):
    count = frames.shape[1]
    joined = jnp.concatenate([earlier, frames], axis=1)
    filtered = jnp.zeros(frames.shape, jnp.float32)
    for tap_index in range(TAPS):
        filtered = filtered + prototype[tap_index] * joined[:, tap_index:tap_index + count, :].astype(jnp.float32)
    filtered = filtered.astype(jnp.bfloat16)
    flat = filtered.reshape(-1, frames.shape[2])
    spectra = jnp.dot(flat, dft_table(frames.shape[2]), preferred_element_type=jnp.float32)
    return spectra.astype(jnp.bfloat16).reshape(frames.shape)

def correlate(planes):
    real_part = planes[0]
    imag_part = planes[1]
    left = jnp.concatenate([real_part, imag_part], axis=1)
    right = jnp.concatenate([imag_part, -real_part], axis=1)
    dims = (((1,), (1,)), ((), ()))
    real_gram = lax.dot_general(left, left, dims, preferred_element_type=jnp.float32)
    imag_gram = lax.dot_general(right, left, dims, preferred_element_type=jnp.float32)
    scales = lax.rsqrt(jnp.diagonal(real_gram) + 1e-06)
    outer = scales[:, None] * scales[None, :]
    return jnp.stack([real_gram * outer, imag_gram * outer]).astype(jnp.bfloat16)

def reference(voltages, prototype):
    block = math.gcd(INPUTS, 64)
    grouped = voltages.reshape(INPUTS // block, block, SPEC, FRAME)

    def one_block(frames):
        earlier = jnp.zeros((block, TAPS - 1, FRAME), jnp.bfloat16)
        return channelize(frames, earlier, prototype)
    spectra = lax.map(one_block, grouped).reshape(INPUTS, SPEC, CHAN, 2)
    planes = spectra.transpose(2, 3, 0, 1)
    return lax.map(correlate, planes)
```

```python
import functools

import jax
import jax.numpy as jnp
import numpy as np
from jax import lax
from jax.experimental import pallas as pl
from jax.experimental.pallas import tpu as pltpu
from jax.sharding import PartitionSpec as P

LANES = 128
ROWS = 16
CHUNK = 4
VMEM = 56 * 1024 * 1024


def shifted(block, axis, distance):
    devices = range(lax.axis_size(axis))
    route = [(i - distance, i) for i in devices if i - distance in devices]
    return lax.ppermute(block, axis, route)


def dft_rows(frame, columns):
    sample = np.arange(frame, dtype=np.int64)[None, :]
    columns = columns[:, None]
    phase = (sample * (columns // 2) % frame) * (2.0 * np.pi / frame)
    table = np.where(columns % 2 == 0, np.cos(phase), -np.sin(phase))
    return jnp.asarray(table.astype(jnp.bfloat16))


def fir(load, store, coefficients, count):
    taps = len(coefficients)
    window = [load(f) for f in range(taps - 1)]
    for s in range(count):
        window.append(load(s + taps - 1))
        total = window[0] * coefficients[0]
        for k in range(1, taps):
            total = total + window[k] * coefficients[k]
        store(s, total)
        window.pop(0)


def main_filter_kernel(taps, frame, spectra, skip, v_ref, p_ref, o_ref):
    @pl.loop(0, frame // LANES)
    def _(block):
        at = pl.multiple_of(block * LANES, LANES)
        lanes = pl.ds(at, LANES)
        coefficients = [
            jnp.broadcast_to(p_ref[pl.ds(k, 1), lanes], (ROWS, LANES)) for k in range(taps)
        ]
        first = skip - taps + 1

        def load(f):
            return v_ref[:, pl.ds((first + f) * frame + at, LANES)].astype(jnp.float32)

        def store(s, value):
            o_ref[skip + s, :, lanes] = value.astype(jnp.bfloat16)

        fir(load, store, coefficients, spectra - skip)


def edge_filter_kernel(taps, frame, skip, v_ref, e_ref, p_ref, a_ref, o_ref):
    del a_ref

    @pl.loop(0, frame // LANES)
    def _(block):
        at = pl.multiple_of(block * LANES, LANES)
        lanes = pl.ds(at, LANES)
        coefficients = [
            jnp.broadcast_to(p_ref[pl.ds(k, 1), lanes], (ROWS, LANES)) for k in range(taps)
        ]

        def load(f):
            if f < taps - 1:
                return e_ref[:, pl.ds(f * frame + at, LANES)].astype(jnp.float32)
            return v_ref[:, pl.ds((f - taps + 1) * frame + at, LANES)].astype(jnp.float32)

        def store(s, value):
            o_ref[s, :, lanes] = value.astype(jnp.bfloat16)

        fir(load, store, coefficients, skip)


def filter_frames(voltages, earlier, prototype):
    inputs, samples = voltages.shape
    taps, frame = prototype.shape
    spectra = samples // frame
    skip = 8
    assert taps - 1 <= skip < spectra
    params = pltpu.CompilerParams(vmem_limit_bytes=VMEM)
    shape = jax.ShapeDtypeStruct((spectra, inputs, frame), jnp.bfloat16)
    partial = pl.pallas_call(
        functools.partial(main_filter_kernel, taps, frame, spectra, skip),
        grid=(inputs // ROWS,),
        in_specs=[
            pl.BlockSpec((ROWS, samples), lambda r: (r, 0)),
            pl.BlockSpec((taps, frame), lambda r: (0, 0)),
        ],
        out_specs=pl.BlockSpec((spectra, ROWS, frame), lambda r: (0, r, 0)),
        out_shape=shape,
        compiler_params=params,
        cost_estimate=pl.CostEstimate(
            flops=2 * taps * inputs * samples,
            bytes_accessed=4 * inputs * samples,
            transcendentals=0,
        ),
        name="filter_main",
    )(voltages, prototype)
    return pl.pallas_call(
        functools.partial(edge_filter_kernel, taps, frame, skip),
        grid=(inputs // ROWS,),
        in_specs=[
            pl.BlockSpec((ROWS, skip * frame), lambda r: (r, 0)),
            pl.BlockSpec((ROWS, (taps - 1) * frame), lambda r: (r, 0)),
            pl.BlockSpec((taps, frame), lambda r: (0, 0)),
            pl.BlockSpec(memory_space=pl.ANY),
        ],
        out_specs=pl.BlockSpec((skip, ROWS, frame), lambda r: (0, r, 0)),
        out_shape=shape,
        input_output_aliases={3: 0},
        compiler_params=params,
        cost_estimate=pl.CostEstimate(
            flops=2 * taps * inputs * skip * frame,
            bytes_accessed=6 * inputs * skip * frame,
            transcendentals=0,
        ),
        name="filter_edge",
    )(voltages, earlier, prototype, partial)


def dft_kernel(columns, inputs, t_ref, f_ref, o_ref, turn):
    group = max(1, 256 // inputs)
    for s in range(0, ROWS, group):
        frames = f_ref[pl.ds(s, group)].reshape(group * inputs, f_ref.shape[2])
        product = lax.dot_general(
            t_ref[...], frames, (((1,), (1,)), ((), ())), preferred_element_type=jnp.float32
        )
        for part in range(group):
            turn[pl.ds(s + part, columns, stride=ROWS), :] = product[
                :, part * inputs : (part + 1) * inputs
            ]
    o_ref[...] = turn[...].reshape(columns, ROWS, inputs).astype(jnp.bfloat16)


def transform(table, filtered):
    spectra, inputs, frame = filtered.shape
    columns = table.shape[0]
    if inputs % LANES:
        dims = (((1,), (2,)), ((), ()))
        out = lax.dot_general(table, filtered, dims, preferred_element_type=jnp.float32)
        return out.astype(jnp.bfloat16)
    return pl.pallas_call(
        functools.partial(dft_kernel, columns, inputs),
        grid=(spectra // ROWS,),
        in_specs=[
            pl.BlockSpec((columns, frame), lambda b: (0, 0)),
            pl.BlockSpec((ROWS, inputs, frame), lambda b: (b, 0, 0)),
        ],
        out_specs=pl.BlockSpec((columns, ROWS, inputs), lambda b: (0, b, 0)),
        out_shape=jax.ShapeDtypeStruct((columns, spectra, inputs), jnp.bfloat16),
        scratch_shapes=[pltpu.VMEM((columns * ROWS, inputs), jnp.float32)],
        compiler_params=pltpu.CompilerParams(vmem_limit_bytes=VMEM),
        cost_estimate=pl.CostEstimate(
            flops=2 * columns * spectra * inputs * frame,
            bytes_accessed=2 * spectra * inputs * (frame + columns),
            transcendentals=0,
        ),
        name="dft",
    )(table, filtered)


def correlate_kernel(block, *refs):
    r_ref, o_ref, right, left = refs[0], refs[-3], refs[-2], refs[-1]
    groups, slabs, _, _, here, width = r_ref.shape
    spectra = slabs * here
    inputs = groups * width
    for part in range(2):
        for t in range(slabs):
            for g in range(groups):
                right[
                    pl.ds(part * spectra + t * here, here), pl.ds(g * width, width)
                ] = r_ref[g, t, 0, part]
    power = jnp.zeros((1, inputs), jnp.float32)
    for at in range(0, 2 * spectra, ROWS):
        piece = right[pl.ds(at, ROWS), :].astype(jnp.float32)
        power = power + jnp.sum(piece * piece, axis=0, keepdims=True)
    across = lax.rsqrt(power + 1e-06)
    left[...] = right[...].T

    @pl.loop(0, inputs // block)
    def _(index):
        rows = pl.ds(pl.multiple_of(index * block, block), block)
        own = left[rows, :]
        wide = own.astype(jnp.float32)
        down = lax.rsqrt(jnp.sum(wide * wide, axis=1, keepdims=True) + 1e-06)
        swapped = jnp.concatenate([own[:, spectra:], -own[:, :spectra]], axis=1)
        for part, operand in enumerate((own, swapped)):
            gram = jnp.dot(operand, right[...], preferred_element_type=jnp.float32)
            o_ref[0, part, rows, :] = (gram * down * across).astype(jnp.bfloat16)


def correlate(pieces, total, first, channels):
    groups, slabs, chunk, _, here, width = pieces.shape
    if width % LANES:
        pieces = pieces.transpose(2, 3, 1, 4, 0, 5)
        pieces = pieces.reshape(1, 1, chunk, 2, slabs * here, groups * width)
        groups, slabs, chunk, _, here, width = pieces.shape
    inputs, spectra = groups * width, slabs * here
    in_specs = [pl.BlockSpec((groups, slabs, 1, 2, here, width), lambda c: (0, 0, c, 0, 0, 0))]
    operands = [pieces]
    aliases = {}
    if total is not None:
        in_specs.append(pl.BlockSpec(memory_space=pl.ANY))
        operands.append(total)
        aliases = {1: 0}
    return pl.pallas_call(
        functools.partial(correlate_kernel, min(256, inputs)),
        grid=(chunk,),
        in_specs=in_specs,
        out_specs=pl.BlockSpec((1, 2, inputs, inputs), lambda c: (first + c, 0, 0, 0)),
        out_shape=jax.ShapeDtypeStruct((channels, 2, inputs, inputs), jnp.bfloat16),
        input_output_aliases=aliases,
        scratch_shapes=[
            pltpu.VMEM((2 * spectra, inputs), jnp.bfloat16),
            pltpu.VMEM((inputs, 2 * spectra), jnp.bfloat16),
        ],
        compiler_params=pltpu.CompilerParams(vmem_limit_bytes=VMEM),
        cost_estimate=pl.CostEstimate(
            flops=8 * chunk * inputs * inputs * spectra,
            bytes_accessed=4 * chunk * inputs * (inputs + spectra),
            transcendentals=0,
        ),
        name="correlate",
    )(*operands)


def shards(voltages, prototype):
    inputs, samples = voltages.shape
    taps, frame = prototype.shape
    spectra = samples // frame
    groups = lax.axis_size("inp")
    slabs = lax.axis_size("tm")
    devices = groups * slabs
    channels = frame // 2 // devices
    chunk = min(CHUNK, channels)
    earlier = shifted(voltages[:, (spectra - taps + 1) * frame :], "tm", 1)
    filtered = filter_frames(voltages, earlier, prototype)
    device = np.arange(devices)[:, None, None]
    total = None
    for first in range(0, channels, chunk):
        channel = device * channels + first + np.arange(chunk)[None, :, None]
        columns = (2 * channel + np.arange(2)[None, None, :]).reshape(-1)
        spectrum = transform(dft_rows(frame, columns), filtered)
        spectrum = spectrum.reshape(devices, 2 * chunk, spectra, inputs)
        turned = lax.all_to_all(
            spectrum, ("inp", "tm"), split_axis=0, concat_axis=0, tiled=True
        )
        pieces = turned.reshape(groups, slabs, chunk, 2, spectra, inputs)
        total = correlate(pieces, total, first, channels)
    return total


def solution(mesh):
    return jax.shard_map(
        shards,
        mesh=mesh,
        in_specs=(P("inp", "tm"), P()),
        out_specs=P(("inp", "tm"), None, None, None),
        check_vma=False,
    )
```

```python
import functools

import jax
import jax.numpy as jnp
import numpy as np
from jax import lax
from jax.experimental import pallas as pl
from jax.experimental.pallas import tpu as pltpu
from jax.sharding import PartitionSpec as P

LANES = 128
ROWS = 16
VMEM = 63 * 1024 * 1024
WEIGHT = 8


def shifted(block, axis, distance):
    devices = range(lax.axis_size(axis))
    route = [(i - distance, i) for i in devices if i - distance in devices]
    return lax.ppermute(block, axis, route)


def dft_rows(frame, columns):
    sample = np.arange(frame, dtype=np.int64)[None, :]
    columns = columns[:, None]
    phase = (sample * (columns // 2) % frame) * (2.0 * np.pi / frame)
    table = np.where(columns % 2 == 0, np.cos(phase), -np.sin(phase))
    return jnp.asarray(table.astype(jnp.bfloat16))


def fir(load, store, coefficients, count):
    taps = len(coefficients)
    window = [load(f) for f in range(taps - 1)]
    for s in range(count):
        window.append(load(s + taps - 1))
        total = window[0] * coefficients[0]
        for k in range(1, taps):
            total = total + window[k] * coefficients[k]
        store(s, total)
        window.pop(0)


def main_filter_kernel(taps, frame, spectra, skip, v_ref, p_ref, o_ref):
    @pl.loop(0, frame // LANES)
    def _(block):
        at = pl.multiple_of(block * LANES, LANES)
        lanes = pl.ds(at, LANES)
        coefficients = [
            jnp.broadcast_to(p_ref[pl.ds(k, 1), lanes], (ROWS, LANES)) for k in range(taps)
        ]
        first = skip - taps + 1

        def load(f):
            return v_ref[:, pl.ds((first + f) * frame + at, LANES)].astype(jnp.float32)

        def store(s, value):
            o_ref[s, :, lanes] = value.astype(jnp.bfloat16)

        fir(load, store, coefficients, spectra - skip)


def edge_filter_kernel(taps, frame, skip, v_ref, e_ref, p_ref, o_ref):
    @pl.loop(0, frame // LANES)
    def _(block):
        at = pl.multiple_of(block * LANES, LANES)
        lanes = pl.ds(at, LANES)
        coefficients = [
            jnp.broadcast_to(p_ref[pl.ds(k, 1), lanes], (ROWS, LANES)) for k in range(taps)
        ]

        def load(f):
            if f < taps - 1:
                return e_ref[:, pl.ds(f * frame + at, LANES)].astype(jnp.float32)
            return v_ref[:, pl.ds((f - taps + 1) * frame + at, LANES)].astype(jnp.float32)

        def store(s, value):
            o_ref[s, :, lanes] = value.astype(jnp.bfloat16)

        fir(load, store, coefficients, skip)


def filter_main(voltages, prototype):
    inputs, samples = voltages.shape
    taps, frame = prototype.shape
    spectra = samples // frame
    assert taps - 1 <= ROWS < spectra
    return pl.pallas_call(
        functools.partial(main_filter_kernel, taps, frame, spectra, ROWS),
        grid=(inputs // ROWS,),
        in_specs=[
            pl.BlockSpec((ROWS, samples), lambda r: (r, 0)),
            pl.BlockSpec((taps, frame), lambda r: (0, 0)),
        ],
        out_specs=pl.BlockSpec((spectra - ROWS, ROWS, frame), lambda r: (0, r, 0)),
        out_shape=jax.ShapeDtypeStruct((spectra - ROWS, inputs, frame), jnp.bfloat16),
        compiler_params=pltpu.CompilerParams(vmem_limit_bytes=VMEM),
        cost_estimate=pl.CostEstimate(
            flops=2 * taps * inputs * samples,
            bytes_accessed=4 * inputs * samples,
            transcendentals=0,
        ),
        name="filter_main",
    )(voltages, prototype)


def filter_edge(voltages, earlier, prototype):
    inputs = voltages.shape[0]
    taps, frame = prototype.shape
    return pl.pallas_call(
        functools.partial(edge_filter_kernel, taps, frame, ROWS),
        grid=(inputs // ROWS,),
        in_specs=[
            pl.BlockSpec((ROWS, ROWS * frame), lambda r: (r, 0)),
            pl.BlockSpec((ROWS, (taps - 1) * frame), lambda r: (r, 0)),
            pl.BlockSpec((taps, frame), lambda r: (0, 0)),
        ],
        out_specs=pl.BlockSpec((ROWS, ROWS, frame), lambda r: (0, r, 0)),
        out_shape=jax.ShapeDtypeStruct((ROWS, inputs, frame), jnp.bfloat16),
        compiler_params=pltpu.CompilerParams(vmem_limit_bytes=VMEM),
        cost_estimate=pl.CostEstimate(
            flops=512 * WEIGHT * taps * inputs * ROWS * frame,
            bytes_accessed=6 * inputs * ROWS * frame,
            transcendentals=0,
        ),
        name="filter_edge",
    )(voltages, earlier, prototype)


def dft_kernel(inputs, t_ref, f_ref, *refs):
    o_ref, turn = refs[-2], refs[-1]
    columns = t_ref.shape[0]
    group = max(1, 256 // inputs)
    for s in range(0, ROWS, group):
        frames = f_ref[pl.ds(s, group)].reshape(group * inputs, f_ref.shape[2])
        product = lax.dot_general(
            t_ref[...], frames, (((1,), (1,)), ((), ())), preferred_element_type=jnp.float32
        )
        for part in range(group):
            turn[pl.ds(s + part, columns, stride=ROWS), :] = product[
                :, part * inputs : (part + 1) * inputs
            ]
    o_ref[...] = turn[...].reshape(o_ref.shape).astype(jnp.bfloat16)


def transform(table, filtered, devices, rows, first, buffer):
    spectra, inputs, frame = filtered.shape
    columns = table.shape[0]
    height = columns // devices * ROWS
    assert first % height == 0
    split = 1
    while columns // split > 320 and devices % (2 * split) == 0:
        split *= 2
    in_specs = [
        pl.BlockSpec((columns // split, frame), lambda b, d: (d, 0)),
        pl.BlockSpec((ROWS, inputs, frame), lambda b, d: (b, 0, 0)),
    ]
    operands = [table, filtered]
    if buffer is not None:
        in_specs.append(pl.BlockSpec(memory_space=pl.ANY))
        operands.append(buffer)
    return pl.pallas_call(
        functools.partial(dft_kernel, inputs),
        grid=(spectra // ROWS, split),
        in_specs=in_specs,
        out_specs=pl.BlockSpec(
            (devices // split, height, inputs), lambda b, d: (d, first // height + b, 0)
        ),
        out_shape=jax.ShapeDtypeStruct((devices, rows, inputs), jnp.bfloat16),
        input_output_aliases={} if buffer is None else {2: 0},
        scratch_shapes=[pltpu.VMEM((columns // split * ROWS, inputs), jnp.float32)],
        compiler_params=pltpu.CompilerParams(vmem_limit_bytes=VMEM),
        cost_estimate=pl.CostEstimate(
            flops=WEIGHT * columns * spectra * inputs * frame,
            bytes_accessed=2 * spectra * inputs * (frame + columns),
            transcendentals=0,
        ),
        name="dft",
    )(*operands)


def correlate_block(block, o_ref, right, left):
    depth, inputs = right.shape
    spectra = depth // 2
    power = jnp.zeros((ROWS, inputs), jnp.float32)
    for at in range(0, depth, ROWS):
        piece = right[pl.ds(at, ROWS), :].astype(jnp.float32)
        power = power + piece * piece
    across = lax.rsqrt(jnp.sum(power, axis=0, keepdims=True) + 1e-06)
    down = jnp.broadcast_to(across, (8, inputs)).T[:, :1]
    left[...] = right[...].T
    for at in range(0, inputs, block):
        rows = pl.ds(at, block)
        own = left[rows, :]
        swapped = jnp.concatenate([own[:, spectra:], -own[:, :spectra]], axis=1)
        for part, operand in enumerate((own, swapped)):
            gram = jnp.dot(operand, right[...], preferred_element_type=jnp.float32)
            o_ref[0, part, rows, :] = (gram * down[at : at + block] * across).astype(jnp.bfloat16)


def correlate_kernel(block, slabs, count, *refs):
    blocks, o_ref, right, left = refs[:count], refs[-3], refs[-2], refs[-1]
    devices, _, width = blocks[0].shape
    spectra = right.shape[0] // 2
    for part in range(2):
        for device in range(devices):
            g, t = device // slabs, device % slabs
            for b, ref in enumerate(blocks):
                at = part * spectra + (t * len(blocks) + b) * ROWS
                right[pl.ds(at, ROWS), pl.ds(g * width, width)] = ref[
                    device, pl.ds(part * ROWS, ROWS), :
                ]
    correlate_block(block, o_ref, right, left)


def plain_correlate_kernel(block, r_ref, o_ref, right, left):
    right[...] = r_ref[0]
    correlate_block(block, o_ref, right, left)


def correlate(kernel, in_specs, operands, total, first, count, out_shape, spectra):
    inputs = out_shape.shape[-1]
    aliases = {}
    if total is not None:
        aliases = {len(operands): 0}
        in_specs = [*in_specs, pl.BlockSpec(memory_space=pl.ANY)]
        operands = [*operands, total]
    return pl.pallas_call(
        kernel,
        grid=(count,),
        in_specs=in_specs,
        out_specs=pl.BlockSpec((1, 2, inputs, inputs), lambda c: (first + c, 0, 0, 0)),
        out_shape=out_shape,
        input_output_aliases=aliases,
        scratch_shapes=[
            pltpu.VMEM((2 * spectra, inputs), jnp.bfloat16),
            pltpu.VMEM((inputs, 2 * spectra), jnp.bfloat16),
        ],
        compiler_params=pltpu.CompilerParams(vmem_limit_bytes=VMEM),
        cost_estimate=pl.CostEstimate(
            flops=8 * count * inputs * inputs * spectra,
            bytes_accessed=4 * count * inputs * (inputs + spectra),
            transcendentals=0,
        ),
        name="correlate",
    )(*operands)


def table_of(frame, devices, channels, first, count):
    channel = np.arange(devices)[:, None, None] * channels + first
    channel = channel + np.arange(count)[None, :, None]
    return dft_rows(frame, (2 * channel + np.arange(2)[None, None, :]).reshape(-1))


def exchange(rows):
    return lax.all_to_all(rows, ("inp", "tm"), split_axis=0, concat_axis=0, tiled=True)


def narrow(voltages, prototype, earlier, out_shape):
    inputs, samples = voltages.shape
    frame = prototype.shape[1]
    groups, slabs = lax.axis_size("inp"), lax.axis_size("tm")
    devices, channels = groups * slabs, out_shape.shape[0]
    spectra = samples // frame
    filtered = jnp.concatenate(
        [filter_edge(voltages, earlier, prototype), filter_main(voltages, prototype)]
    )
    table = table_of(frame, devices, channels, 0, channels)
    dims = (((1,), (2,)), ((), ()))
    rows = lax.dot_general(table, filtered, dims, preferred_element_type=jnp.float32)
    rows = rows.astype(jnp.bfloat16).reshape(devices, -1, inputs)
    turned = exchange(rows).reshape(groups, slabs, channels, 2, spectra, inputs)
    depth = 2 * slabs * spectra
    planes = turned.transpose(2, 3, 1, 4, 0, 5).reshape(channels, depth, groups * inputs)
    return correlate(
        functools.partial(plain_correlate_kernel, min(256, groups * inputs)),
        [pl.BlockSpec((1, depth, groups * inputs), lambda c: (c, 0, 0))],
        [planes],
        None,
        0,
        channels,
        out_shape,
        depth // 2,
    )


def shards(voltages, prototype):
    inputs, samples = voltages.shape
    taps, frame = prototype.shape
    spectra = samples // frame
    groups, slabs = lax.axis_size("inp"), lax.axis_size("tm")
    devices = groups * slabs
    channels = frame // 2 // devices
    total_inputs = groups * inputs
    out_shape = jax.ShapeDtypeStruct((channels, 2, total_inputs, total_inputs), jnp.bfloat16)
    earlier = shifted(voltages[:, (spectra - taps + 1) * frame :], "tm", 1)
    if inputs % LANES or channels % 16:
        return narrow(voltages, prototype, earlier, out_shape)

    middle = channels // 2
    last = 3 * channels // 16
    early = channels - middle - last
    blocks = spectra // ROWS
    unit = 2 * ROWS

    main = filter_main(voltages, prototype)
    rows = (blocks - 1) * early * unit
    table = table_of(frame, devices, channels, 0, early)
    first_turned = exchange(transform(table, main, devices, rows, 0, None))

    edge = filter_edge(voltages, earlier, prototype)
    rows = channels * unit + (blocks - 1) * middle * unit
    table = table_of(frame, devices, channels, 0, channels)
    buffer = transform(table, edge, devices, rows, 0, None)
    table = table_of(frame, devices, channels, early, middle)
    buffer = transform(table, main, devices, rows, channels * unit, buffer)
    middle_turned = exchange(buffer)

    rows = (blocks - 1) * last * unit
    table = table_of(frame, devices, channels, early + middle, last)
    last_turned = exchange(transform(table, main, devices, rows, 0, None))

    total = None
    first = 0
    for turned, count, base in (
        (first_turned, early, 0),
        (middle_turned, middle, channels),
        (last_turned, last, 0),
    ):
        shape = (devices, unit, inputs)
        in_specs = [pl.BlockSpec(shape, lambda c, first=first: (0, first + c, 0))]
        for b in range(blocks - 1):
            at = base + b * count
            in_specs.append(pl.BlockSpec(shape, lambda c, at=at: (0, at + c, 0)))
        operands = [middle_turned] + [turned] * (blocks - 1)
        kernel = functools.partial(correlate_kernel, min(256, total_inputs), slabs, blocks)
        total = correlate(
            kernel, in_specs, operands, total, first, count, out_shape, slabs * spectra
        )
        first += count
    return total


def solution(mesh):
    return jax.shard_map(
        shards,
        mesh=mesh,
        in_specs=(P("inp", "tm"), P()),
        out_specs=P(("inp", "tm"), None, None, None),
        check_vma=False,
    )
```

```python
import functools

import jax
import jax.numpy as jnp
import numpy as np
from jax import lax
from jax.experimental import pallas as pl
from jax.experimental.pallas import tpu as pltpu
from jax.sharding import PartitionSpec as P

LANES = 128
ROWS = 16
VMEM = 63 * 1024 * 1024
VMEM_FIRST = 56 * 1024 * 1024
WEIGHT = 8


def shifted(block, axis, distance):
    devices = range(lax.axis_size(axis))
    route = [(i - distance, i) for i in devices if i - distance in devices]
    return lax.ppermute(block, axis, route)


def dft_rows(frame, columns):
    sample = np.arange(frame, dtype=np.int64)[None, :]
    columns = columns[:, None]
    phase = (sample * (columns // 2) % frame) * (2.0 * np.pi / frame)
    table = np.where(columns % 2 == 0, np.cos(phase), -np.sin(phase))
    return jnp.asarray(table.astype(jnp.bfloat16))


def fir(load, store, coefficients, count):
    taps = len(coefficients)
    window = [load(f) for f in range(taps - 1)]
    for s in range(count):
        window.append(load(s + taps - 1))
        total = window[0] * coefficients[0]
        for k in range(1, taps):
            total = total + window[k] * coefficients[k]
        store(s, total)
        window.pop(0)


def main_filter_kernel(taps, frame, spectra, skip, v_ref, p_ref, o_ref):
    @pl.loop(0, frame // LANES)
    def _(block):
        at = pl.multiple_of(block * LANES, LANES)
        lanes = pl.ds(at, LANES)
        coefficients = [
            jnp.broadcast_to(p_ref[pl.ds(k, 1), lanes], (ROWS, LANES)) for k in range(taps)
        ]
        first = skip - taps + 1

        def load(f):
            return v_ref[:, pl.ds((first + f) * frame + at, LANES)].astype(jnp.float32)

        def store(s, value):
            o_ref[s, :, lanes] = value.astype(jnp.bfloat16)

        fir(load, store, coefficients, spectra - skip)


def edge_filter_kernel(taps, frame, skip, v_ref, e_ref, p_ref, o_ref):
    @pl.loop(0, frame // LANES)
    def _(block):
        at = pl.multiple_of(block * LANES, LANES)
        lanes = pl.ds(at, LANES)
        coefficients = [
            jnp.broadcast_to(p_ref[pl.ds(k, 1), lanes], (ROWS, LANES)) for k in range(taps)
        ]

        def load(f):
            if f < taps - 1:
                return e_ref[:, pl.ds(f * frame + at, LANES)].astype(jnp.float32)
            return v_ref[:, pl.ds((f - taps + 1) * frame + at, LANES)].astype(jnp.float32)

        def store(s, value):
            o_ref[s, :, lanes] = value.astype(jnp.bfloat16)

        fir(load, store, coefficients, skip)


def filter_main(voltages, prototype):
    inputs, samples = voltages.shape
    taps, frame = prototype.shape
    spectra = samples // frame
    assert taps - 1 <= ROWS < spectra
    return pl.pallas_call(
        functools.partial(main_filter_kernel, taps, frame, spectra, ROWS),
        grid=(inputs // ROWS,),
        in_specs=[
            pl.BlockSpec((ROWS, samples), lambda r: (r, 0)),
            pl.BlockSpec((taps, frame), lambda r: (0, 0)),
        ],
        out_specs=pl.BlockSpec((spectra - ROWS, ROWS, frame), lambda r: (0, r, 0)),
        out_shape=jax.ShapeDtypeStruct((spectra - ROWS, inputs, frame), jnp.bfloat16),
        compiler_params=pltpu.CompilerParams(vmem_limit_bytes=VMEM_FIRST),
        cost_estimate=pl.CostEstimate(
            flops=2 * taps * inputs * samples,
            bytes_accessed=4 * inputs * samples,
            transcendentals=0,
        ),
        name="filter_main",
    )(voltages, prototype)


def filter_edge(voltages, earlier, prototype):
    inputs = voltages.shape[0]
    taps, frame = prototype.shape
    return pl.pallas_call(
        functools.partial(edge_filter_kernel, taps, frame, ROWS),
        grid=(inputs // ROWS,),
        in_specs=[
            pl.BlockSpec((ROWS, ROWS * frame), lambda r: (r, 0)),
            pl.BlockSpec((ROWS, (taps - 1) * frame), lambda r: (r, 0)),
            pl.BlockSpec((taps, frame), lambda r: (0, 0)),
        ],
        out_specs=pl.BlockSpec((ROWS, ROWS, frame), lambda r: (0, r, 0)),
        out_shape=jax.ShapeDtypeStruct((ROWS, inputs, frame), jnp.bfloat16),
        compiler_params=pltpu.CompilerParams(vmem_limit_bytes=VMEM),
        cost_estimate=pl.CostEstimate(
            flops=512 * WEIGHT * taps * inputs * ROWS * frame,
            bytes_accessed=6 * inputs * ROWS * frame,
            transcendentals=0,
        ),
        name="filter_edge",
    )(voltages, earlier, prototype)


def dft_kernel(inputs, t_ref, f_ref, *refs):
    o_ref, turn = refs[-2], refs[-1]
    columns = t_ref.shape[0]
    group = max(1, 256 // inputs)
    for s in range(0, ROWS, group):
        frames = f_ref[pl.ds(s, group)].reshape(group * inputs, f_ref.shape[2])
        product = lax.dot_general(
            t_ref[...], frames, (((1,), (1,)), ((), ())), preferred_element_type=jnp.float32
        )
        for part in range(group):
            turn[pl.ds(s + part, columns, stride=ROWS), :] = product[
                :, part * inputs : (part + 1) * inputs
            ]
    o_ref[...] = turn[...].reshape(o_ref.shape).astype(jnp.bfloat16)


def transform(table, filtered, devices, rows, first, buffer, vmem=VMEM):
    spectra, inputs, frame = filtered.shape
    columns = table.shape[0]
    height = columns // devices * ROWS
    assert first % height == 0
    split = 1
    while columns // split > 384 and devices % (2 * split) == 0:
        split *= 2
    in_specs = [
        pl.BlockSpec((columns // split, frame), lambda b, d: (d, 0)),
        pl.BlockSpec((ROWS, inputs, frame), lambda b, d: (b, 0, 0)),
    ]
    operands = [table, filtered]
    if buffer is not None:
        in_specs.append(pl.BlockSpec(memory_space=pl.ANY))
        operands.append(buffer)
    return pl.pallas_call(
        functools.partial(dft_kernel, inputs),
        grid=(spectra // ROWS, split),
        in_specs=in_specs,
        out_specs=pl.BlockSpec(
            (devices // split, height, inputs), lambda b, d: (d, first // height + b, 0)
        ),
        out_shape=jax.ShapeDtypeStruct((devices, rows, inputs), jnp.bfloat16),
        input_output_aliases={} if buffer is None else {2: 0},
        scratch_shapes=[pltpu.VMEM((columns // split * ROWS, inputs), jnp.float32)],
        compiler_params=pltpu.CompilerParams(vmem_limit_bytes=vmem),
        cost_estimate=pl.CostEstimate(
            flops=WEIGHT * columns * spectra * inputs * frame,
            bytes_accessed=2 * spectra * inputs * (frame + columns),
            transcendentals=0,
        ),
        name="dft",
    )(*operands)


def pipelined(block, count, fill, o_ref, slots):
    step = pl.program_id(0)
    depth, inputs = slots[0][0].shape
    spectra = depth // 2

    def prepare(at, slot):
        right, left, across = slot
        columns = pl.ds(at, block)
        fill(at, right)
        power = jnp.zeros((ROWS, block), jnp.float32)
        for row in range(0, depth, ROWS):
            piece = right[pl.ds(row, ROWS), columns].astype(jnp.float32)
            power = power + piece * piece
        scale = lax.rsqrt(jnp.sum(power, axis=0, keepdims=True) + 1e-06)
        across[:, columns] = jnp.broadcast_to(scale, (8, block))
        left[columns, :] = right[:, columns].T

    def multiply(at, slot):
        right, left, across = slot
        rows = pl.ds(at, block)
        own = left[rows, :]
        swapped = jnp.concatenate([own[:, spectra:], -own[:, :spectra]], axis=1)
        down = across[:, rows].T[:, :1]
        for part, operand in enumerate((own, swapped)):
            gram = jnp.dot(operand, right[...], preferred_element_type=jnp.float32)
            o_ref[0, part, rows, :] = (gram * down * across[:1, :]).astype(jnp.bfloat16)

    def both(old, new):
        for at in range(0, inputs, block):
            if old is not None:
                multiply(at, old)
            if new is not None:
                prepare(at, new)

    even, odd = slots
    inside = (step > 0) & (step < count)
    pl.when(step == 0)(lambda: both(None, even))
    pl.when(inside & (step % 2 == 1))(lambda: both(even, odd))
    pl.when(inside & (step % 2 == 0))(lambda: both(odd, even))
    pl.when(step == count)(lambda: both(slots[(count - 1) % 2], None))


def correlate_kernel(block, count, slabs, blocks, *refs):
    sources, o_ref, slots = refs[:blocks], refs[-7], (refs[-6:-3], refs[-3:])
    devices, _, width = sources[0].shape
    spectra = slots[0][0].shape[0] // 2

    def fill(first, right):
        for part in range(2):
            for device in range(first // width * slabs, (first + block) // width * slabs):
                g, t = device // slabs, device % slabs
                for b, ref in enumerate(sources):
                    at = part * spectra + (t * blocks + b) * ROWS
                    right[pl.ds(at, ROWS), pl.ds(g * width, width)] = ref[
                        device, pl.ds(part * ROWS, ROWS), :
                    ]

    pipelined(block, count, fill, o_ref, slots)


def plain_correlate_kernel(block, count, r_ref, o_ref, *scratch):
    def fill(first, right):
        columns = pl.ds(first, block)
        right[:, columns] = r_ref[0, :, columns]

    pipelined(block, count, fill, o_ref, (scratch[:3], scratch[3:]))


def correlate(kernel, in_specs, operands, total, first, count, out_shape, spectra):
    inputs = out_shape.shape[-1]
    aliases = {}
    if total is not None:
        aliases = {len(operands): 0}
        in_specs = [*in_specs, pl.BlockSpec(memory_space=pl.ANY)]
        operands = [*operands, total]
    slot = [
        pltpu.VMEM((2 * spectra, inputs), jnp.bfloat16),
        pltpu.VMEM((inputs, 2 * spectra), jnp.bfloat16),
        pltpu.VMEM((8, inputs), jnp.float32),
    ]
    return pl.pallas_call(
        kernel,
        grid=(count + 1,),
        in_specs=in_specs,
        out_specs=pl.BlockSpec(
            (1, 2, inputs, inputs), lambda c: (first + jnp.maximum(c - 1, 0), 0, 0, 0)
        ),
        out_shape=out_shape,
        input_output_aliases=aliases,
        scratch_shapes=slot + slot,
        compiler_params=pltpu.CompilerParams(vmem_limit_bytes=VMEM),
        cost_estimate=pl.CostEstimate(
            flops=8 * count * inputs * inputs * spectra,
            bytes_accessed=4 * count * inputs * (inputs + spectra),
            transcendentals=0,
        ),
        name="correlate",
    )(*operands)


def table_of(frame, devices, channels, first, count):
    channel = np.arange(devices)[:, None, None] * channels + first
    channel = channel + np.arange(count)[None, :, None]
    return dft_rows(frame, (2 * channel + np.arange(2)[None, None, :]).reshape(-1))


def exchange(rows):
    return lax.all_to_all(rows, ("inp", "tm"), split_axis=0, concat_axis=0, tiled=True)


def narrow(voltages, prototype, earlier, out_shape):
    inputs, samples = voltages.shape
    frame = prototype.shape[1]
    groups, slabs = lax.axis_size("inp"), lax.axis_size("tm")
    devices, channels = groups * slabs, out_shape.shape[0]
    spectra = samples // frame
    filtered = jnp.concatenate(
        [filter_edge(voltages, earlier, prototype), filter_main(voltages, prototype)]
    )
    table = table_of(frame, devices, channels, 0, channels)
    dims = (((1,), (2,)), ((), ()))
    rows = lax.dot_general(table, filtered, dims, preferred_element_type=jnp.float32)
    rows = rows.astype(jnp.bfloat16).reshape(devices, -1, inputs)
    turned = exchange(rows).reshape(groups, slabs, channels, 2, spectra, inputs)
    depth = 2 * slabs * spectra
    planes = turned.transpose(2, 3, 1, 4, 0, 5).reshape(channels, depth, groups * inputs)
    return correlate(
        functools.partial(plain_correlate_kernel, min(256, groups * inputs), channels),
        [
            pl.BlockSpec(
                (1, depth, groups * inputs), lambda c: (jnp.minimum(c, channels - 1), 0, 0)
            )
        ],
        [planes],
        None,
        0,
        channels,
        out_shape,
        depth // 2,
    )


def shards(voltages, prototype):
    inputs, samples = voltages.shape
    taps, frame = prototype.shape
    spectra = samples // frame
    groups, slabs = lax.axis_size("inp"), lax.axis_size("tm")
    devices = groups * slabs
    channels = frame // 2 // devices
    total_inputs = groups * inputs
    out_shape = jax.ShapeDtypeStruct((channels, 2, total_inputs, total_inputs), jnp.bfloat16)
    earlier = shifted(voltages[:, (spectra - taps + 1) * frame :], "tm", 1)
    if inputs % LANES or channels % 16:
        return narrow(voltages, prototype, earlier, out_shape)

    middle = channels // 2
    last = channels // 8
    early = channels - middle - last
    blocks = spectra // ROWS
    unit = 2 * ROWS

    main = filter_main(voltages, prototype)
    rows = (blocks - 1) * early * unit
    table = table_of(frame, devices, channels, 0, early)
    first_turned = exchange(transform(table, main, devices, rows, 0, None, VMEM_FIRST))

    edge = filter_edge(voltages, earlier, prototype)
    rows = channels * unit + (blocks - 1) * middle * unit
    table = table_of(frame, devices, channels, 0, channels)
    buffer = transform(table, edge, devices, rows, 0, None)
    table = table_of(frame, devices, channels, early, middle)
    buffer = transform(table, main, devices, rows, channels * unit, buffer)
    middle_turned = exchange(buffer)

    rows = (blocks - 1) * last * unit
    table = table_of(frame, devices, channels, early + middle, last)
    last_turned = exchange(transform(table, main, devices, rows, 0, None))

    total = None
    first = 0
    for turned, count, base in (
        (first_turned, early, 0),
        (middle_turned, middle, channels),
        (last_turned, last, 0),
    ):
        bases = [first] + [base + b * count for b in range(blocks - 1)]
        in_specs = [
            pl.BlockSpec(
                (devices, unit, inputs),
                lambda c, at=at, end=count - 1: (0, at + jnp.minimum(c, end), 0),
            )
            for at in bases
        ]
        operands = [middle_turned] + [turned] * (blocks - 1)
        kernel = functools.partial(
            correlate_kernel, min(256, total_inputs), count, slabs, blocks
        )
        total = correlate(
            kernel, in_specs, operands, total, first, count, out_shape, slabs * spectra
        )
        first += count
    return total


def solution(mesh):
    return jax.shard_map(
        shards,
        mesh=mesh,
        in_specs=(P("inp", "tm"), P()),
        out_specs=P(("inp", "tm"), None, None, None),
        check_vma=False,
    )
```

```python
import functools

import jax
import jax.numpy as jnp
import numpy as np
from jax import lax
from jax.experimental import pallas as pl
from jax.experimental.pallas import tpu as pltpu
from jax.sharding import PartitionSpec as P

LANES = 128
ROWS = 16
VMEM = 63 * 1024 * 1024
VMEM_FIRST = 56 * 1024 * 1024
WEIGHT = 8


def shifted(block, axis, distance):
    devices = range(lax.axis_size(axis))
    route = [(i - distance, i) for i in devices if i - distance in devices]
    return lax.ppermute(block, axis, route)


def dft_rows(frame, columns):
    sample = np.arange(frame, dtype=np.int64)[None, :]
    columns = columns[:, None]
    phase = (sample * (columns // 2) % frame) * (2.0 * np.pi / frame)
    table = np.where(columns % 2 == 0, np.cos(phase), -np.sin(phase))
    return jnp.asarray(table.astype(jnp.bfloat16))


def fir(load, store, coefficients, count):
    taps = len(coefficients)
    window = [load(f) for f in range(taps - 1)]
    for s in range(count):
        window.append(load(s + taps - 1))
        total = window[0] * coefficients[0]
        for k in range(1, taps):
            total = total + window[k] * coefficients[k]
        store(s, total)
        window.pop(0)


def main_filter_kernel(taps, frame, spectra, skip, v_ref, p_ref, o_ref):
    @pl.loop(0, frame // LANES)
    def _(block):
        at = pl.multiple_of(block * LANES, LANES)
        lanes = pl.ds(at, LANES)
        coefficients = [
            jnp.broadcast_to(p_ref[pl.ds(k, 1), lanes], (ROWS, LANES)) for k in range(taps)
        ]
        first = skip - taps + 1

        def load(f):
            return v_ref[:, pl.ds((first + f) * frame + at, LANES)].astype(jnp.float32)

        def store(s, value):
            o_ref[s, :, lanes] = value.astype(jnp.bfloat16)

        fir(load, store, coefficients, spectra - skip)


def edge_filter_kernel(taps, frame, skip, v_ref, e_ref, p_ref, o_ref):
    @pl.loop(0, frame // LANES)
    def _(block):
        at = pl.multiple_of(block * LANES, LANES)
        lanes = pl.ds(at, LANES)
        coefficients = [
            jnp.broadcast_to(p_ref[pl.ds(k, 1), lanes], (ROWS, LANES)) for k in range(taps)
        ]

        def load(f):
            if f < taps - 1:
                return e_ref[:, pl.ds(f * frame + at, LANES)].astype(jnp.float32)
            return v_ref[:, pl.ds((f - taps + 1) * frame + at, LANES)].astype(jnp.float32)

        def store(s, value):
            o_ref[s, :, lanes] = value.astype(jnp.bfloat16)

        fir(load, store, coefficients, skip)


def filter_main(voltages, prototype):
    inputs, samples = voltages.shape
    taps, frame = prototype.shape
    spectra = samples // frame
    assert taps - 1 <= ROWS < spectra
    return pl.pallas_call(
        functools.partial(main_filter_kernel, taps, frame, spectra, ROWS),
        grid=(inputs // ROWS,),
        in_specs=[
            pl.BlockSpec((ROWS, samples), lambda r: (r, 0)),
            pl.BlockSpec((taps, frame), lambda r: (0, 0)),
        ],
        out_specs=pl.BlockSpec((spectra - ROWS, ROWS, frame), lambda r: (0, r, 0)),
        out_shape=jax.ShapeDtypeStruct((spectra - ROWS, inputs, frame), jnp.bfloat16),
        compiler_params=pltpu.CompilerParams(vmem_limit_bytes=VMEM_FIRST),
        cost_estimate=pl.CostEstimate(
            flops=2 * taps * inputs * samples,
            bytes_accessed=4 * inputs * samples,
            transcendentals=0,
        ),
        name="filter_main",
    )(voltages, prototype)


def filter_edge(voltages, earlier, prototype):
    inputs = voltages.shape[0]
    taps, frame = prototype.shape
    return pl.pallas_call(
        functools.partial(edge_filter_kernel, taps, frame, ROWS),
        grid=(inputs // ROWS,),
        in_specs=[
            pl.BlockSpec((ROWS, ROWS * frame), lambda r: (r, 0)),
            pl.BlockSpec((ROWS, (taps - 1) * frame), lambda r: (r, 0)),
            pl.BlockSpec((taps, frame), lambda r: (0, 0)),
        ],
        out_specs=pl.BlockSpec((ROWS, ROWS, frame), lambda r: (0, r, 0)),
        out_shape=jax.ShapeDtypeStruct((ROWS, inputs, frame), jnp.bfloat16),
        compiler_params=pltpu.CompilerParams(vmem_limit_bytes=VMEM),
        cost_estimate=pl.CostEstimate(
            flops=512 * WEIGHT * taps * inputs * ROWS * frame,
            bytes_accessed=6 * inputs * ROWS * frame,
            transcendentals=0,
        ),
        name="filter_edge",
    )(voltages, earlier, prototype)


def dft_kernel(inputs, t_ref, f_ref, *refs):
    o_ref, turn = refs[-2], refs[-1]
    columns = t_ref.shape[0]
    group = max(1, 256 // inputs)
    for s in range(0, ROWS, group):
        frames = f_ref[pl.ds(s, group)].reshape(group * inputs, f_ref.shape[2])
        product = lax.dot_general(
            t_ref[...], frames, (((1,), (1,)), ((), ())), preferred_element_type=jnp.float32
        )
        for part in range(group):
            turn[pl.ds(s + part, columns, stride=ROWS), :] = product[
                :, part * inputs : (part + 1) * inputs
            ]
    o_ref[...] = turn[...].reshape(o_ref.shape).astype(jnp.bfloat16)


def transform(table, filtered, devices, rows, first, buffer, vmem=VMEM):
    spectra, inputs, frame = filtered.shape
    columns = table.shape[0]
    height = columns // devices * ROWS
    assert first % height == 0
    split = 1
    while columns // split > 384 and devices % (2 * split) == 0:
        split *= 2
    in_specs = [
        pl.BlockSpec((columns // split, frame), lambda b, d: (d, 0)),
        pl.BlockSpec((ROWS, inputs, frame), lambda b, d: (b, 0, 0)),
    ]
    operands = [table, filtered]
    if buffer is not None:
        in_specs.append(pl.BlockSpec(memory_space=pl.ANY))
        operands.append(buffer)
    return pl.pallas_call(
        functools.partial(dft_kernel, inputs),
        grid=(spectra // ROWS, split),
        in_specs=in_specs,
        out_specs=pl.BlockSpec(
            (devices // split, height, inputs), lambda b, d: (d, first // height + b, 0)
        ),
        out_shape=jax.ShapeDtypeStruct((devices, rows, inputs), jnp.bfloat16),
        input_output_aliases={} if buffer is None else {2: 0},
        scratch_shapes=[pltpu.VMEM((columns // split * ROWS, inputs), jnp.float32)],
        compiler_params=pltpu.CompilerParams(vmem_limit_bytes=vmem),
        cost_estimate=pl.CostEstimate(
            flops=WEIGHT * columns * spectra * inputs * frame,
            bytes_accessed=2 * spectra * inputs * (frame + columns),
            transcendentals=0,
        ),
        name="dft",
    )(*operands)


def pipelined(block, count, fill, o_ref, slots):
    step = pl.program_id(0)
    depth, inputs = slots[0][0].shape
    spectra = depth // 2

    def prepare(at, slot):
        right, left, across = slot
        columns = pl.ds(at, block)
        fill(at, right)
        power = jnp.zeros((ROWS, block), jnp.float32)
        for row in range(0, depth, ROWS):
            piece = right[pl.ds(row, ROWS), columns].astype(jnp.float32)
            power = power + piece * piece
        scale = lax.rsqrt(jnp.sum(power, axis=0, keepdims=True) + 1e-06)
        across[:, columns] = jnp.broadcast_to(scale, (8, block))
        left[columns, :] = right[:, columns].T

    def multiply(at, slot):
        right, left, across = slot
        rows, columns = pl.ds(at, block), pl.ds(at, inputs - at)
        own = left[rows, :]
        swapped = jnp.concatenate([own[:, spectra:], -own[:, :spectra]], axis=1)
        down = across[:, rows].T[:, :1]
        for part, operand in enumerate((own, swapped)):
            gram = jnp.dot(operand, right[:, columns], preferred_element_type=jnp.float32)
            scaled = (gram * down * across[:1, columns]).astype(jnp.bfloat16)
            o_ref[0, part, rows, columns] = scaled
            for below in range(at + block, inputs, block):
                mirror = scaled[:, below - at : below - at + block].T
                o_ref[0, part, pl.ds(below, block), rows] = -mirror if part else mirror

    def both(old, new):
        for at in range(0, inputs, block):
            if old is not None:
                multiply(at, old)
            if new is not None:
                prepare(at, new)

    even, odd = slots
    inside = (step > 0) & (step < count)
    pl.when(step == 0)(lambda: both(None, even))
    pl.when(inside & (step % 2 == 1))(lambda: both(even, odd))
    pl.when(inside & (step % 2 == 0))(lambda: both(odd, even))
    pl.when(step == count)(lambda: both(slots[(count - 1) % 2], None))


def correlate_kernel(block, count, slabs, blocks, *refs):
    sources, o_ref, slots = refs[:blocks], refs[-7], (refs[-6:-3], refs[-3:])
    devices, _, width = sources[0].shape
    spectra = slots[0][0].shape[0] // 2

    def fill(first, right):
        for part in range(2):
            for device in range(first // width * slabs, (first + block) // width * slabs):
                g, t = device // slabs, device % slabs
                for b, ref in enumerate(sources):
                    at = part * spectra + (t * blocks + b) * ROWS
                    right[pl.ds(at, ROWS), pl.ds(g * width, width)] = ref[
                        device, pl.ds(part * ROWS, ROWS), :
                    ]

    pipelined(block, count, fill, o_ref, slots)


def plain_correlate_kernel(block, count, r_ref, o_ref, *scratch):
    def fill(first, right):
        columns = pl.ds(first, block)
        right[:, columns] = r_ref[0, :, columns]

    pipelined(block, count, fill, o_ref, (scratch[:3], scratch[3:]))


def correlate(kernel, in_specs, operands, total, first, count, out_shape, spectra):
    inputs = out_shape.shape[-1]
    aliases = {}
    if total is not None:
        aliases = {len(operands): 0}
        in_specs = [*in_specs, pl.BlockSpec(memory_space=pl.ANY)]
        operands = [*operands, total]
    slot = [
        pltpu.VMEM((2 * spectra, inputs), jnp.bfloat16),
        pltpu.VMEM((inputs, 2 * spectra), jnp.bfloat16),
        pltpu.VMEM((8, inputs), jnp.float32),
    ]
    return pl.pallas_call(
        kernel,
        grid=(count + 1,),
        in_specs=in_specs,
        out_specs=pl.BlockSpec(
            (1, 2, inputs, inputs), lambda c: (first + jnp.maximum(c - 1, 0), 0, 0, 0)
        ),
        out_shape=out_shape,
        input_output_aliases=aliases,
        scratch_shapes=slot + slot,
        compiler_params=pltpu.CompilerParams(vmem_limit_bytes=VMEM),
        cost_estimate=pl.CostEstimate(
            flops=8 * count * inputs * inputs * spectra,
            bytes_accessed=4 * count * inputs * (inputs + spectra),
            transcendentals=0,
        ),
        name="correlate",
    )(*operands)


def table_of(frame, devices, channels, first, count):
    channel = np.arange(devices)[:, None, None] * channels + first
    channel = channel + np.arange(count)[None, :, None]
    return dft_rows(frame, (2 * channel + np.arange(2)[None, None, :]).reshape(-1))


def exchange(rows):
    return lax.all_to_all(rows, ("inp", "tm"), split_axis=0, concat_axis=0, tiled=True)


def narrow(voltages, prototype, earlier, out_shape):
    inputs, samples = voltages.shape
    frame = prototype.shape[1]
    groups, slabs = lax.axis_size("inp"), lax.axis_size("tm")
    devices, channels = groups * slabs, out_shape.shape[0]
    spectra = samples // frame
    filtered = jnp.concatenate(
        [filter_edge(voltages, earlier, prototype), filter_main(voltages, prototype)]
    )
    table = table_of(frame, devices, channels, 0, channels)
    dims = (((1,), (2,)), ((), ()))
    rows = lax.dot_general(table, filtered, dims, preferred_element_type=jnp.float32)
    rows = rows.astype(jnp.bfloat16).reshape(devices, -1, inputs)
    turned = exchange(rows).reshape(groups, slabs, channels, 2, spectra, inputs)
    depth = 2 * slabs * spectra
    planes = turned.transpose(2, 3, 1, 4, 0, 5).reshape(channels, depth, groups * inputs)
    return correlate(
        functools.partial(plain_correlate_kernel, min(256, groups * inputs), channels),
        [
            pl.BlockSpec(
                (1, depth, groups * inputs), lambda c: (jnp.minimum(c, channels - 1), 0, 0)
            )
        ],
        [planes],
        None,
        0,
        channels,
        out_shape,
        depth // 2,
    )


def shards(voltages, prototype):
    inputs, samples = voltages.shape
    taps, frame = prototype.shape
    spectra = samples // frame
    groups, slabs = lax.axis_size("inp"), lax.axis_size("tm")
    devices = groups * slabs
    channels = frame // 2 // devices
    total_inputs = groups * inputs
    out_shape = jax.ShapeDtypeStruct((channels, 2, total_inputs, total_inputs), jnp.bfloat16)
    earlier = shifted(voltages[:, (spectra - taps + 1) * frame :], "tm", 1)
    if inputs % LANES or channels % 16:
        return narrow(voltages, prototype, earlier, out_shape)

    middle = channels // 2
    last = channels // 8
    early = channels - middle - last
    blocks = spectra // ROWS
    unit = 2 * ROWS

    main = filter_main(voltages, prototype)
    rows = (blocks - 1) * early * unit
    table = table_of(frame, devices, channels, 0, early)
    first_turned = exchange(transform(table, main, devices, rows, 0, None, VMEM_FIRST))

    edge = filter_edge(voltages, earlier, prototype)
    rows = channels * unit + (blocks - 1) * middle * unit
    table = table_of(frame, devices, channels, 0, channels)
    buffer = transform(table, edge, devices, rows, 0, None)
    table = table_of(frame, devices, channels, early, middle)
    buffer = transform(table, main, devices, rows, channels * unit, buffer)
    middle_turned = exchange(buffer)

    rows = (blocks - 1) * last * unit
    table = table_of(frame, devices, channels, early + middle, last)
    last_turned = exchange(transform(table, main, devices, rows, 0, None))

    total = None
    first = 0
    for turned, count, base in (
        (first_turned, early, 0),
        (middle_turned, middle, channels),
        (last_turned, last, 0),
    ):
        bases = [first] + [base + b * count for b in range(blocks - 1)]
        in_specs = [
            pl.BlockSpec(
                (devices, unit, inputs),
                lambda c, at=at, end=count - 1: (0, at + jnp.minimum(c, end), 0),
            )
            for at in bases
        ]
        operands = [middle_turned] + [turned] * (blocks - 1)
        kernel = functools.partial(
            correlate_kernel, min(256, total_inputs), count, slabs, blocks
        )
        total = correlate(
            kernel, in_specs, operands, total, first, count, out_shape, slabs * spectra
        )
        first += count
    return total


def solution(mesh):
    return jax.shard_map(
        shards,
        mesh=mesh,
        in_specs=(P("inp", "tm"), P()),
        out_specs=P(("inp", "tm"), None, None, None),
        check_vma=False,
    )
```

```python
import functools

import jax
import jax.numpy as jnp
import numpy as np
from jax import lax
from jax.experimental import pallas as pl
from jax.experimental.pallas import tpu as pltpu
from jax.sharding import PartitionSpec as P

LANES = 128
ROWS = 16
VMEM = 63 * 1024 * 1024
VMEM_FIRST = 56 * 1024 * 1024
WEIGHT = 8


def shifted(block, axis, distance):
    devices = range(lax.axis_size(axis))
    route = [(i - distance, i) for i in devices if i - distance in devices]
    return lax.ppermute(block, axis, route)


def dft_rows(frame, columns):
    sample = np.arange(frame, dtype=np.int64)[None, :]
    columns = columns[:, None]
    phase = (sample * (columns // 2) % frame) * (2.0 * np.pi / frame)
    table = np.where(columns % 2 == 0, np.cos(phase), -np.sin(phase))
    return jnp.asarray(table.astype(jnp.bfloat16))


def fir(load, store, coefficients, count):
    taps = len(coefficients)
    window = [load(f) for f in range(taps - 1)]
    for s in range(count):
        window.append(load(s + taps - 1))
        total = window[0] * coefficients[0]
        for k in range(1, taps):
            total = total + window[k] * coefficients[k]
        store(s, total)
        window.pop(0)


def main_filter_kernel(taps, frame, spectra, skip, v_ref, p_ref, o_ref):
    @pl.loop(0, frame // LANES)
    def _(block):
        at = pl.multiple_of(block * LANES, LANES)
        lanes = pl.ds(at, LANES)
        coefficients = [
            jnp.broadcast_to(p_ref[pl.ds(k, 1), lanes], (ROWS, LANES)) for k in range(taps)
        ]
        first = skip - taps + 1

        def load(f):
            return v_ref[:, pl.ds((first + f) * frame + at, LANES)].astype(jnp.float32)

        def store(s, value):
            o_ref[s, :, lanes] = value.astype(jnp.bfloat16)

        fir(load, store, coefficients, spectra - skip)


def edge_filter_kernel(taps, frame, skip, v_ref, e_ref, p_ref, o_ref):
    @pl.loop(0, frame // LANES)
    def _(block):
        at = pl.multiple_of(block * LANES, LANES)
        lanes = pl.ds(at, LANES)
        coefficients = [
            jnp.broadcast_to(p_ref[pl.ds(k, 1), lanes], (ROWS, LANES)) for k in range(taps)
        ]

        def load(f):
            if f < taps - 1:
                return e_ref[:, pl.ds(f * frame + at, LANES)].astype(jnp.float32)
            return v_ref[:, pl.ds((f - taps + 1) * frame + at, LANES)].astype(jnp.float32)

        def store(s, value):
            o_ref[s, :, lanes] = value.astype(jnp.bfloat16)

        fir(load, store, coefficients, skip)


def filter_main(voltages, prototype):
    inputs, samples = voltages.shape
    taps, frame = prototype.shape
    spectra = samples // frame
    assert taps - 1 <= ROWS < spectra
    return pl.pallas_call(
        functools.partial(main_filter_kernel, taps, frame, spectra, ROWS),
        grid=(inputs // ROWS,),
        in_specs=[
            pl.BlockSpec((ROWS, samples), lambda r: (r, 0)),
            pl.BlockSpec((taps, frame), lambda r: (0, 0)),
        ],
        out_specs=pl.BlockSpec((spectra - ROWS, ROWS, frame), lambda r: (0, r, 0)),
        out_shape=jax.ShapeDtypeStruct((spectra - ROWS, inputs, frame), jnp.bfloat16),
        compiler_params=pltpu.CompilerParams(vmem_limit_bytes=VMEM_FIRST),
        cost_estimate=pl.CostEstimate(
            flops=2 * taps * inputs * samples,
            bytes_accessed=4 * inputs * samples,
            transcendentals=0,
        ),
        name="filter_main",
    )(voltages, prototype)


def filter_edge(voltages, earlier, prototype):
    inputs = voltages.shape[0]
    taps, frame = prototype.shape
    return pl.pallas_call(
        functools.partial(edge_filter_kernel, taps, frame, ROWS),
        grid=(inputs // ROWS,),
        in_specs=[
            pl.BlockSpec((ROWS, ROWS * frame), lambda r: (r, 0)),
            pl.BlockSpec((ROWS, (taps - 1) * frame), lambda r: (r, 0)),
            pl.BlockSpec((taps, frame), lambda r: (0, 0)),
        ],
        out_specs=pl.BlockSpec((ROWS, ROWS, frame), lambda r: (0, r, 0)),
        out_shape=jax.ShapeDtypeStruct((ROWS, inputs, frame), jnp.bfloat16),
        compiler_params=pltpu.CompilerParams(vmem_limit_bytes=VMEM),
        cost_estimate=pl.CostEstimate(
            flops=512 * WEIGHT * taps * inputs * ROWS * frame,
            bytes_accessed=6 * inputs * ROWS * frame,
            transcendentals=0,
        ),
        name="filter_edge",
    )(voltages, earlier, prototype)


def dft_kernel(inputs, t_ref, f_ref, *refs):
    o_ref, turn = refs[-2], refs[-1]
    columns = t_ref.shape[0]
    group = max(1, 256 // inputs)
    for s in range(0, ROWS, group):
        frames = f_ref[pl.ds(s, group)].reshape(group * inputs, f_ref.shape[2])
        product = lax.dot_general(
            t_ref[...], frames, (((1,), (1,)), ((), ())), preferred_element_type=jnp.float32
        )
        for part in range(group):
            turn[pl.ds(s + part, columns, stride=ROWS), :] = product[
                :, part * inputs : (part + 1) * inputs
            ]
    o_ref[...] = turn[...].reshape(o_ref.shape).astype(jnp.bfloat16)


def transform(table, filtered, devices, rows, first, buffer, vmem=VMEM):
    spectra, inputs, frame = filtered.shape
    columns = table.shape[0]
    height = columns // devices * ROWS
    assert first % height == 0
    split = 1
    while columns // split > 384 and devices % (2 * split) == 0:
        split *= 2
    in_specs = [
        pl.BlockSpec((columns // split, frame), lambda b, d: (d, 0)),
        pl.BlockSpec((ROWS, inputs, frame), lambda b, d: (b, 0, 0)),
    ]
    operands = [table, filtered]
    if buffer is not None:
        in_specs.append(pl.BlockSpec(memory_space=pl.ANY))
        operands.append(buffer)
    return pl.pallas_call(
        functools.partial(dft_kernel, inputs),
        grid=(spectra // ROWS, split),
        in_specs=in_specs,
        out_specs=pl.BlockSpec(
            (devices // split, height, inputs), lambda b, d: (d, first // height + b, 0)
        ),
        out_shape=jax.ShapeDtypeStruct((devices, rows, inputs), jnp.bfloat16),
        input_output_aliases={} if buffer is None else {2: 0},
        scratch_shapes=[pltpu.VMEM((columns // split * ROWS, inputs), jnp.float32)],
        compiler_params=pltpu.CompilerParams(vmem_limit_bytes=vmem),
        cost_estimate=pl.CostEstimate(
            flops=WEIGHT * columns * spectra * inputs * frame,
            bytes_accessed=2 * spectra * inputs * (frame + columns),
            transcendentals=0,
        ),
        name="dft",
    )(*operands)


def pipelined(block, count, fill, o_ref, slots):
    step = pl.program_id(0)
    depth, inputs = slots[0][0].shape
    spectra = depth // 2

    def prepare(at, slot):
        right, left, across = slot
        columns = pl.ds(at, block)
        fill(at, right)
        power = jnp.zeros((ROWS, block), jnp.float32)
        for row in range(0, depth, ROWS):
            piece = right[pl.ds(row, ROWS), columns].astype(jnp.float32)
            power = power + piece * piece
        scale = lax.rsqrt(jnp.sum(power, axis=0, keepdims=True) + 1e-06)
        across[:, columns] = jnp.broadcast_to(scale, (8, block))
        turned = right[:, columns].T
        left[pl.ds(2 * at, block), :] = turned
        left[pl.ds(2 * at + block, block), pl.ds(0, spectra)] = turned[:, spectra:]
        left[pl.ds(2 * at + block, block), pl.ds(spectra, spectra)] = -turned[:, :spectra]

    def multiply(at, slot):
        right, left, across = slot
        rows = pl.ds(at, block)
        operand = left[pl.ds(2 * at, 2 * block), :]
        down = across[:, rows].T[:, :1]
        for other in range(at, inputs, block):
            columns = pl.ds(other, block)
            gram = jnp.dot(operand, right[:, columns], preferred_element_type=jnp.float32)
            for part in range(2):
                own = gram[part * block : (part + 1) * block]
                scaled = (own * down * across[:1, columns]).astype(jnp.bfloat16)
                o_ref[0, part, rows, columns] = scaled
                if other > at:
                    o_ref[0, part, columns, rows] = -scaled.T if part else scaled.T

    def both(old, new):
        for at in range(0, inputs, block):
            if old is not None:
                multiply(at, old)
            if new is not None:
                prepare(at, new)

    even, odd = slots
    inside = (step > 0) & (step < count)
    pl.when(step == 0)(lambda: both(None, even))
    pl.when(inside & (step % 2 == 1))(lambda: both(even, odd))
    pl.when(inside & (step % 2 == 0))(lambda: both(odd, even))
    pl.when(step == count)(lambda: both(slots[(count - 1) % 2], None))


def correlate_kernel(block, count, slabs, blocks, *refs):
    sources, o_ref, slots = refs[:blocks], refs[-7], (refs[-6:-3], refs[-3:])
    devices, _, width = sources[0].shape
    spectra = slots[0][0].shape[0] // 2

    def fill(first, right):
        for part in range(2):
            for device in range(first // width * slabs, (first + block) // width * slabs):
                g, t = device // slabs, device % slabs
                for b, ref in enumerate(sources):
                    at = part * spectra + (t * blocks + b) * ROWS
                    right[pl.ds(at, ROWS), pl.ds(g * width, width)] = ref[
                        device, pl.ds(part * ROWS, ROWS), :
                    ]

    pipelined(block, count, fill, o_ref, slots)


def plain_correlate_kernel(block, count, r_ref, o_ref, *scratch):
    def fill(first, right):
        columns = pl.ds(first, block)
        right[:, columns] = r_ref[0, :, columns]

    pipelined(block, count, fill, o_ref, (scratch[:3], scratch[3:]))


def correlate(kernel, in_specs, operands, total, first, count, out_shape, spectra):
    inputs = out_shape.shape[-1]
    aliases = {}
    if total is not None:
        aliases = {len(operands): 0}
        in_specs = [*in_specs, pl.BlockSpec(memory_space=pl.ANY)]
        operands = [*operands, total]
    slot = [
        pltpu.VMEM((2 * spectra, inputs), jnp.bfloat16),
        pltpu.VMEM((2 * inputs, 2 * spectra), jnp.bfloat16),
        pltpu.VMEM((8, inputs), jnp.float32),
    ]
    return pl.pallas_call(
        kernel,
        grid=(count + 1,),
        in_specs=in_specs,
        out_specs=pl.BlockSpec(
            (1, 2, inputs, inputs), lambda c: (first + jnp.maximum(c - 1, 0), 0, 0, 0)
        ),
        out_shape=out_shape,
        input_output_aliases=aliases,
        scratch_shapes=slot + slot,
        compiler_params=pltpu.CompilerParams(vmem_limit_bytes=VMEM),
        cost_estimate=pl.CostEstimate(
            flops=8 * count * inputs * inputs * spectra,
            bytes_accessed=4 * count * inputs * (inputs + spectra),
            transcendentals=0,
        ),
        name="correlate",
    )(*operands)


def table_of(frame, devices, channels, first, count):
    channel = np.arange(devices)[:, None, None] * channels + first
    channel = channel + np.arange(count)[None, :, None]
    return dft_rows(frame, (2 * channel + np.arange(2)[None, None, :]).reshape(-1))


def exchange(rows):
    return lax.all_to_all(rows, ("inp", "tm"), split_axis=0, concat_axis=0, tiled=True)


def narrow(voltages, prototype, earlier, out_shape):
    inputs, samples = voltages.shape
    frame = prototype.shape[1]
    groups, slabs = lax.axis_size("inp"), lax.axis_size("tm")
    devices, channels = groups * slabs, out_shape.shape[0]
    spectra = samples // frame
    filtered = jnp.concatenate(
        [filter_edge(voltages, earlier, prototype), filter_main(voltages, prototype)]
    )
    table = table_of(frame, devices, channels, 0, channels)
    dims = (((1,), (2,)), ((), ()))
    rows = lax.dot_general(table, filtered, dims, preferred_element_type=jnp.float32)
    rows = rows.astype(jnp.bfloat16).reshape(devices, -1, inputs)
    turned = exchange(rows).reshape(groups, slabs, channels, 2, spectra, inputs)
    depth = 2 * slabs * spectra
    planes = turned.transpose(2, 3, 1, 4, 0, 5).reshape(channels, depth, groups * inputs)
    return correlate(
        functools.partial(plain_correlate_kernel, min(256, groups * inputs), channels),
        [
            pl.BlockSpec(
                (1, depth, groups * inputs), lambda c: (jnp.minimum(c, channels - 1), 0, 0)
            )
        ],
        [planes],
        None,
        0,
        channels,
        out_shape,
        depth // 2,
    )


def shards(voltages, prototype):
    inputs, samples = voltages.shape
    taps, frame = prototype.shape
    spectra = samples // frame
    groups, slabs = lax.axis_size("inp"), lax.axis_size("tm")
    devices = groups * slabs
    channels = frame // 2 // devices
    total_inputs = groups * inputs
    out_shape = jax.ShapeDtypeStruct((channels, 2, total_inputs, total_inputs), jnp.bfloat16)
    earlier = shifted(voltages[:, (spectra - taps + 1) * frame :], "tm", 1)
    if inputs % LANES or channels % 16:
        return narrow(voltages, prototype, earlier, out_shape)

    middle = channels // 2
    last = channels // 8
    early = channels - middle - last
    blocks = spectra // ROWS
    unit = 2 * ROWS

    main = filter_main(voltages, prototype)
    rows = (blocks - 1) * early * unit
    table = table_of(frame, devices, channels, 0, early)
    first_turned = exchange(transform(table, main, devices, rows, 0, None, VMEM_FIRST))

    edge = filter_edge(voltages, earlier, prototype)
    rows = channels * unit + (blocks - 1) * middle * unit
    table = table_of(frame, devices, channels, 0, channels)
    buffer = transform(table, edge, devices, rows, 0, None)
    table = table_of(frame, devices, channels, early, middle)
    buffer = transform(table, main, devices, rows, channels * unit, buffer)
    middle_turned = exchange(buffer)

    rows = (blocks - 1) * last * unit
    table = table_of(frame, devices, channels, early + middle, last)
    last_turned = exchange(transform(table, main, devices, rows, 0, None))

    total = None
    first = 0
    for turned, count, base in (
        (first_turned, early, 0),
        (middle_turned, middle, channels),
        (last_turned, last, 0),
    ):
        bases = [first] + [base + b * count for b in range(blocks - 1)]
        in_specs = [
            pl.BlockSpec(
                (devices, unit, inputs),
                lambda c, at=at, end=count - 1: (0, at + jnp.minimum(c, end), 0),
            )
            for at in bases
        ]
        operands = [middle_turned] + [turned] * (blocks - 1)
        kernel = functools.partial(
            correlate_kernel, min(256, total_inputs), count, slabs, blocks
        )
        total = correlate(
            kernel, in_specs, operands, total, first, count, out_shape, slabs * spectra
        )
        first += count
    return total


def solution(mesh):
    return jax.shard_map(
        shards,
        mesh=mesh,
        in_specs=(P("inp", "tm"), P()),
        out_specs=P(("inp", "tm"), None, None, None),
        check_vma=False,
    )
```

```python
import functools

import jax
import jax.numpy as jnp
import numpy as np
from jax import lax
from jax.experimental import pallas as pl
from jax.experimental.pallas import tpu as pltpu
from jax.sharding import PartitionSpec as P

LANES = 128
ROWS = 16
VMEM = 63 * 1024 * 1024
VMEM_FIRST = 56 * 1024 * 1024
WEIGHT = 8


def shifted(block, axis, distance):
    devices = range(lax.axis_size(axis))
    route = [(i - distance, i) for i in devices if i - distance in devices]
    return lax.ppermute(block, axis, route)


def dft_rows(frame, columns):
    sample = np.arange(frame, dtype=np.int64)[None, :]
    columns = columns[:, None]
    phase = (sample * (columns // 2) % frame) * (2.0 * np.pi / frame)
    table = np.where(columns % 2 == 0, np.cos(phase), -np.sin(phase))
    return jnp.asarray(table.astype(jnp.bfloat16))


def fir(load, store, coefficients, count):
    taps = len(coefficients)
    window = [load(f) for f in range(taps - 1)]
    for s in range(count):
        window.append(load(s + taps - 1))
        total = window[0] * coefficients[0]
        for k in range(1, taps):
            total = total + window[k] * coefficients[k]
        store(s, total)
        window.pop(0)


def main_filter_kernel(taps, frame, spectra, skip, v_ref, p_ref, o_ref):
    @pl.loop(0, frame // LANES)
    def _(block):
        at = pl.multiple_of(block * LANES, LANES)
        lanes = pl.ds(at, LANES)
        coefficients = [
            jnp.broadcast_to(p_ref[pl.ds(k, 1), lanes], (ROWS, LANES)) for k in range(taps)
        ]
        first = skip - taps + 1

        def load(f):
            return v_ref[:, pl.ds((first + f) * frame + at, LANES)].astype(jnp.float32)

        def store(s, value):
            o_ref[s, :, lanes] = value.astype(jnp.bfloat16)

        fir(load, store, coefficients, spectra - skip)


def edge_filter_kernel(taps, frame, skip, v_ref, e_ref, p_ref, o_ref):
    @pl.loop(0, frame // LANES)
    def _(block):
        at = pl.multiple_of(block * LANES, LANES)
        lanes = pl.ds(at, LANES)
        coefficients = [
            jnp.broadcast_to(p_ref[pl.ds(k, 1), lanes], (ROWS, LANES)) for k in range(taps)
        ]

        def load(f):
            if f < taps - 1:
                return e_ref[:, pl.ds(f * frame + at, LANES)].astype(jnp.float32)
            return v_ref[:, pl.ds((f - taps + 1) * frame + at, LANES)].astype(jnp.float32)

        def store(s, value):
            o_ref[s, :, lanes] = value.astype(jnp.bfloat16)

        fir(load, store, coefficients, skip)


def filter_main(voltages, prototype):
    inputs, samples = voltages.shape
    taps, frame = prototype.shape
    spectra = samples // frame
    assert taps - 1 <= ROWS < spectra
    return pl.pallas_call(
        functools.partial(main_filter_kernel, taps, frame, spectra, ROWS),
        grid=(inputs // ROWS,),
        in_specs=[
            pl.BlockSpec((ROWS, samples), lambda r: (r, 0)),
            pl.BlockSpec((taps, frame), lambda r: (0, 0)),
        ],
        out_specs=pl.BlockSpec((spectra - ROWS, ROWS, frame), lambda r: (0, r, 0)),
        out_shape=jax.ShapeDtypeStruct((spectra - ROWS, inputs, frame), jnp.bfloat16),
        compiler_params=pltpu.CompilerParams(vmem_limit_bytes=VMEM_FIRST),
        cost_estimate=pl.CostEstimate(
            flops=2 * taps * inputs * samples,
            bytes_accessed=4 * inputs * samples,
            transcendentals=0,
        ),
        name="filter_main",
    )(voltages, prototype)


def filter_edge(voltages, earlier, prototype):
    inputs = voltages.shape[0]
    taps, frame = prototype.shape
    return pl.pallas_call(
        functools.partial(edge_filter_kernel, taps, frame, ROWS),
        grid=(inputs // ROWS,),
        in_specs=[
            pl.BlockSpec((ROWS, ROWS * frame), lambda r: (r, 0)),
            pl.BlockSpec((ROWS, (taps - 1) * frame), lambda r: (r, 0)),
            pl.BlockSpec((taps, frame), lambda r: (0, 0)),
        ],
        out_specs=pl.BlockSpec((ROWS, ROWS, frame), lambda r: (0, r, 0)),
        out_shape=jax.ShapeDtypeStruct((ROWS, inputs, frame), jnp.bfloat16),
        compiler_params=pltpu.CompilerParams(vmem_limit_bytes=VMEM),
        cost_estimate=pl.CostEstimate(
            flops=512 * WEIGHT * taps * inputs * ROWS * frame,
            bytes_accessed=6 * inputs * ROWS * frame,
            transcendentals=0,
        ),
        name="filter_edge",
    )(voltages, earlier, prototype)


def dft_kernel(inputs, t_ref, f_ref, *refs):
    o_ref, turn = refs[-2], refs[-1]
    columns = t_ref.shape[0]
    group = max(1, 256 // inputs)
    for s in range(0, ROWS, group):
        frames = f_ref[pl.ds(s, group)].reshape(group * inputs, f_ref.shape[2])
        product = lax.dot_general(
            t_ref[...], frames, (((1,), (1,)), ((), ())), preferred_element_type=jnp.float32
        )
        for part in range(group):
            turn[pl.ds(s + part, columns, stride=ROWS), :] = product[
                :, part * inputs : (part + 1) * inputs
            ]
    o_ref[...] = turn[...].reshape(o_ref.shape).astype(jnp.bfloat16)


def transform(table, filtered, devices, rows, first, buffer, vmem=VMEM):
    spectra, inputs, frame = filtered.shape
    columns = table.shape[0]
    height = columns // devices * ROWS
    assert first % height == 0
    split = 1
    while columns // split > 384 and devices % (2 * split) == 0:
        split *= 2
    in_specs = [
        pl.BlockSpec((columns // split, frame), lambda b, d: (d, 0)),
        pl.BlockSpec((ROWS, inputs, frame), lambda b, d: (b, 0, 0)),
    ]
    operands = [table, filtered]
    if buffer is not None:
        in_specs.append(pl.BlockSpec(memory_space=pl.ANY))
        operands.append(buffer)
    return pl.pallas_call(
        functools.partial(dft_kernel, inputs),
        grid=(spectra // ROWS, split),
        in_specs=in_specs,
        out_specs=pl.BlockSpec(
            (devices // split, height, inputs), lambda b, d: (d, first // height + b, 0)
        ),
        out_shape=jax.ShapeDtypeStruct((devices, rows, inputs), jnp.bfloat16),
        input_output_aliases={} if buffer is None else {2: 0},
        scratch_shapes=[pltpu.VMEM((columns // split * ROWS, inputs), jnp.float32)],
        compiler_params=pltpu.CompilerParams(vmem_limit_bytes=vmem),
        cost_estimate=pl.CostEstimate(
            flops=WEIGHT * columns * spectra * inputs * frame,
            bytes_accessed=2 * spectra * inputs * (frame + columns),
            transcendentals=0,
        ),
        name="dft",
    )(*operands)


def pipelined(block, count, fill, o_ref, slots):
    step = pl.program_id(0)
    depth, inputs = slots[0][0].shape
    spectra = depth // 2

    def prepare(at, slot):
        right, left, across = slot
        columns = pl.ds(at, block)
        fill(at, right)
        power = jnp.zeros((ROWS, block), jnp.float32)
        for row in range(0, depth, ROWS):
            piece = right[pl.ds(row, ROWS), columns].astype(jnp.float32)
            power = power + piece * piece
        scale = lax.rsqrt(jnp.sum(power, axis=0, keepdims=True) + 1e-06)
        across[:, columns] = jnp.broadcast_to(scale, (8, block))
        left[columns, :] = right[:, columns].T

    def multiply(at, slot):
        right, left, across = slot
        rows, columns = pl.ds(at, block), pl.ds(at, inputs - at)
        own = left[rows, :]
        swapped = jnp.concatenate([own[:, spectra:], -own[:, :spectra]], axis=1)
        down = across[:, rows].T[:, :1]
        for part, operand in enumerate((own, swapped)):
            gram = jnp.dot(operand, right[:, columns], preferred_element_type=jnp.float32)
            scaled = (gram * down * across[:1, columns]).astype(jnp.bfloat16)
            o_ref[0, part, rows, columns] = scaled
            for below in range(at + block, inputs, block):
                mirror = scaled[:, below - at : below - at + block].T
                o_ref[0, part, pl.ds(below, block), rows] = -mirror if part else mirror

    def both(old, new):
        for at in range(0, inputs, block):
            if old is not None:
                multiply(at, old)
            if new is not None:
                prepare(at, new)

    even, odd = slots
    inside = (step > 0) & (step < count)
    pl.when(step == 0)(lambda: both(None, even))
    pl.when(inside & (step % 2 == 1))(lambda: both(even, odd))
    pl.when(inside & (step % 2 == 0))(lambda: both(odd, even))
    pl.when(step == count)(lambda: both(slots[(count - 1) % 2], None))


def correlate_kernel(block, count, slabs, blocks, *refs):
    sources, o_ref, slots = refs[:blocks], refs[-7], (refs[-6:-3], refs[-3:])
    devices, _, width = sources[0].shape
    groups = devices // slabs
    spectra = slots[0][0].shape[0] // 2

    def fill(first, right):
        for part in range(2):
            for g in range(first // width, (first + block) // width):
                for t in range(slabs):
                    for b, ref in enumerate(sources):
                        at = part * spectra + (t * blocks + b) * ROWS
                        right[pl.ds(at, ROWS), pl.ds(g * width, width)] = ref[
                            t * groups + g, pl.ds(part * ROWS, ROWS), :
                        ]

    pipelined(block, count, fill, o_ref, slots)


def plain_correlate_kernel(block, count, r_ref, o_ref, *scratch):
    def fill(first, right):
        columns = pl.ds(first, block)
        right[:, columns] = r_ref[0, :, columns]

    pipelined(block, count, fill, o_ref, (scratch[:3], scratch[3:]))


def correlate(kernel, in_specs, operands, total, first, count, out_shape, spectra):
    inputs = out_shape.shape[-1]
    aliases = {}
    if total is not None:
        aliases = {len(operands): 0}
        in_specs = [*in_specs, pl.BlockSpec(memory_space=pl.ANY)]
        operands = [*operands, total]
    slot = [
        pltpu.VMEM((2 * spectra, inputs), jnp.bfloat16),
        pltpu.VMEM((inputs, 2 * spectra), jnp.bfloat16),
        pltpu.VMEM((8, inputs), jnp.float32),
    ]
    return pl.pallas_call(
        kernel,
        grid=(count + 1,),
        in_specs=in_specs,
        out_specs=pl.BlockSpec(
            (1, 2, inputs, inputs), lambda c: (first + jnp.maximum(c - 1, 0), 0, 0, 0)
        ),
        out_shape=out_shape,
        input_output_aliases=aliases,
        scratch_shapes=slot + slot,
        compiler_params=pltpu.CompilerParams(vmem_limit_bytes=VMEM),
        cost_estimate=pl.CostEstimate(
            flops=8 * count * inputs * inputs * spectra,
            bytes_accessed=4 * count * inputs * (inputs + spectra),
            transcendentals=0,
        ),
        name="correlate",
    )(*operands)


def table_of(frame, groups, slabs, channels, first, count):
    device = np.arange(groups)[None, :] * slabs + np.arange(slabs)[:, None]
    channel = device.reshape(-1, 1, 1) * channels + first
    channel = channel + np.arange(count)[None, :, None]
    return dft_rows(frame, (2 * channel + np.arange(2)[None, None, :]).reshape(-1))


def exchange(rows):
    return lax.all_to_all(rows, ("tm", "inp"), split_axis=0, concat_axis=0, tiled=True)


def narrow(voltages, prototype, earlier, out_shape):
    inputs, samples = voltages.shape
    frame = prototype.shape[1]
    groups, slabs = lax.axis_size("inp"), lax.axis_size("tm")
    devices, channels = groups * slabs, out_shape.shape[0]
    spectra = samples // frame
    filtered = jnp.concatenate(
        [filter_edge(voltages, earlier, prototype), filter_main(voltages, prototype)]
    )
    table = table_of(frame, groups, slabs, channels, 0, channels)
    dims = (((1,), (2,)), ((), ()))
    rows = lax.dot_general(table, filtered, dims, preferred_element_type=jnp.float32)
    rows = rows.astype(jnp.bfloat16).reshape(devices, -1, inputs)
    turned = exchange(rows).reshape(slabs, groups, channels, 2, spectra, inputs)
    depth = 2 * slabs * spectra
    planes = turned.transpose(2, 3, 0, 4, 1, 5).reshape(channels, depth, groups * inputs)
    return correlate(
        functools.partial(plain_correlate_kernel, min(256, groups * inputs), channels),
        [
            pl.BlockSpec(
                (1, depth, groups * inputs), lambda c: (jnp.minimum(c, channels - 1), 0, 0)
            )
        ],
        [planes],
        None,
        0,
        channels,
        out_shape,
        depth // 2,
    )


def shards(voltages, prototype):
    inputs, samples = voltages.shape
    taps, frame = prototype.shape
    spectra = samples // frame
    groups, slabs = lax.axis_size("inp"), lax.axis_size("tm")
    devices = groups * slabs
    channels = frame // 2 // devices
    total_inputs = groups * inputs
    out_shape = jax.ShapeDtypeStruct((channels, 2, total_inputs, total_inputs), jnp.bfloat16)
    earlier = shifted(voltages[:, (spectra - taps + 1) * frame :], "tm", 1)
    if inputs % LANES or channels % 16:
        return narrow(voltages, prototype, earlier, out_shape)

    middle = channels // 2
    last = channels // 8
    early = channels - middle - last
    blocks = spectra // ROWS
    unit = 2 * ROWS

    main = filter_main(voltages, prototype)
    rows = (blocks - 1) * early * unit
    table = table_of(frame, groups, slabs, channels, 0, early)
    first_turned = exchange(transform(table, main, devices, rows, 0, None, VMEM_FIRST))

    edge = filter_edge(voltages, earlier, prototype)
    rows = channels * unit + (blocks - 1) * middle * unit
    table = table_of(frame, groups, slabs, channels, 0, channels)
    buffer = transform(table, edge, devices, rows, 0, None)
    table = table_of(frame, groups, slabs, channels, early, middle)
    buffer = transform(table, main, devices, rows, channels * unit, buffer)
    middle_turned = exchange(buffer)

    rows = (blocks - 1) * last * unit
    table = table_of(frame, groups, slabs, channels, early + middle, last)
    last_turned = exchange(transform(table, main, devices, rows, 0, None))

    total = None
    first = 0
    for turned, count, base in (
        (first_turned, early, 0),
        (middle_turned, middle, channels),
        (last_turned, last, 0),
    ):
        bases = [first] + [base + b * count for b in range(blocks - 1)]
        in_specs = [
            pl.BlockSpec(
                (devices, unit, inputs),
                lambda c, at=at, end=count - 1: (0, at + jnp.minimum(c, end), 0),
            )
            for at in bases
        ]
        operands = [middle_turned] + [turned] * (blocks - 1)
        kernel = functools.partial(
            correlate_kernel, min(256, total_inputs), count, slabs, blocks
        )
        total = correlate(
            kernel, in_specs, operands, total, first, count, out_shape, slabs * spectra
        )
        first += count
    return total


def solution(mesh):
    return jax.shard_map(
        shards,
        mesh=mesh,
        in_specs=(P("inp", "tm"), P()),
        out_specs=P(("inp", "tm"), None, None, None),
        check_vma=False,
    )
```

```python
import functools

import jax
import jax.numpy as jnp
import numpy as np
from jax import lax
from jax.experimental import pallas as pl
from jax.experimental.pallas import tpu as pltpu
from jax.sharding import PartitionSpec as P

LANES = 128
ROWS = 16
VMEM = 63 * 1024 * 1024
VMEM_FIRST = 56 * 1024 * 1024
WEIGHT = 8


def shifted(block, axis, distance):
    devices = range(lax.axis_size(axis))
    route = [(i - distance, i) for i in devices if i - distance in devices]
    return lax.ppermute(block, axis, route)


def dft_rows(frame, columns):
    sample = np.arange(frame, dtype=np.int64)[None, :]
    columns = columns[:, None]
    phase = (sample * (columns // 2) % frame) * (2.0 * np.pi / frame)
    table = np.where(columns % 2 == 0, np.cos(phase), -np.sin(phase))
    return jnp.asarray(table.astype(jnp.bfloat16))


def fir(load, store, coefficients, count):
    taps = len(coefficients)
    window = [load(f) for f in range(taps - 1)]
    for s in range(count):
        window.append(load(s + taps - 1))
        total = window[0] * coefficients[0]
        for k in range(1, taps):
            total = total + window[k] * coefficients[k]
        store(s, total)
        window.pop(0)


def main_filter_kernel(taps, frame, spectra, skip, v_ref, p_ref, o_ref):
    @pl.loop(0, frame // LANES)
    def _(block):
        at = pl.multiple_of(block * LANES, LANES)
        lanes = pl.ds(at, LANES)
        coefficients = [
            jnp.broadcast_to(p_ref[pl.ds(k, 1), lanes], (ROWS, LANES)) for k in range(taps)
        ]
        first = skip - taps + 1

        def load(f):
            return v_ref[:, pl.ds((first + f) * frame + at, LANES)].astype(jnp.float32)

        def store(s, value):
            o_ref[s, :, lanes] = value.astype(jnp.bfloat16)

        fir(load, store, coefficients, spectra - skip)


def edge_filter_kernel(taps, frame, skip, v_ref, e_ref, p_ref, o_ref):
    @pl.loop(0, frame // LANES)
    def _(block):
        at = pl.multiple_of(block * LANES, LANES)
        lanes = pl.ds(at, LANES)
        coefficients = [
            jnp.broadcast_to(p_ref[pl.ds(k, 1), lanes], (ROWS, LANES)) for k in range(taps)
        ]

        def load(f):
            if f < taps - 1:
                return e_ref[:, pl.ds(f * frame + at, LANES)].astype(jnp.float32)
            return v_ref[:, pl.ds((f - taps + 1) * frame + at, LANES)].astype(jnp.float32)

        def store(s, value):
            o_ref[s, :, lanes] = value.astype(jnp.bfloat16)

        fir(load, store, coefficients, skip)


def filter_main(voltages, prototype):
    inputs, samples = voltages.shape
    taps, frame = prototype.shape
    spectra = samples // frame
    assert taps - 1 <= ROWS < spectra
    return pl.pallas_call(
        functools.partial(main_filter_kernel, taps, frame, spectra, ROWS),
        grid=(inputs // ROWS,),
        in_specs=[
            pl.BlockSpec((ROWS, samples), lambda r: (r, 0)),
            pl.BlockSpec((taps, frame), lambda r: (0, 0)),
        ],
        out_specs=pl.BlockSpec((spectra - ROWS, ROWS, frame), lambda r: (0, r, 0)),
        out_shape=jax.ShapeDtypeStruct((spectra - ROWS, inputs, frame), jnp.bfloat16),
        compiler_params=pltpu.CompilerParams(vmem_limit_bytes=VMEM_FIRST),
        cost_estimate=pl.CostEstimate(
            flops=2 * taps * inputs * samples,
            bytes_accessed=4 * inputs * samples,
            transcendentals=0,
        ),
        name="filter_main",
    )(voltages, prototype)


def filter_edge(voltages, earlier, prototype):
    inputs = voltages.shape[0]
    taps, frame = prototype.shape
    return pl.pallas_call(
        functools.partial(edge_filter_kernel, taps, frame, ROWS),
        grid=(inputs // ROWS,),
        in_specs=[
            pl.BlockSpec((ROWS, ROWS * frame), lambda r: (r, 0)),
            pl.BlockSpec((ROWS, (taps - 1) * frame), lambda r: (r, 0)),
            pl.BlockSpec((taps, frame), lambda r: (0, 0)),
        ],
        out_specs=pl.BlockSpec((ROWS, ROWS, frame), lambda r: (0, r, 0)),
        out_shape=jax.ShapeDtypeStruct((ROWS, inputs, frame), jnp.bfloat16),
        compiler_params=pltpu.CompilerParams(vmem_limit_bytes=VMEM),
        cost_estimate=pl.CostEstimate(
            flops=512 * WEIGHT * taps * inputs * ROWS * frame,
            bytes_accessed=6 * inputs * ROWS * frame,
            transcendentals=0,
        ),
        name="filter_edge",
    )(voltages, earlier, prototype)


def dft_kernel(inputs, t_ref, f_ref, *refs):
    o_ref, turn = refs[-2], refs[-1]
    columns = t_ref.shape[0]
    group = max(1, 256 // inputs)
    for s in range(0, ROWS, group):
        frames = f_ref[pl.ds(s, group)].reshape(group * inputs, f_ref.shape[2])
        product = lax.dot_general(
            t_ref[...], frames, (((1,), (1,)), ((), ())), preferred_element_type=jnp.float32
        )
        for part in range(group):
            turn[pl.ds(s + part, columns, stride=ROWS), :] = product[
                :, part * inputs : (part + 1) * inputs
            ]
    o_ref[...] = turn[...].reshape(o_ref.shape).astype(jnp.bfloat16)


def transform(table, filtered, devices, rows, first, buffer, vmem=VMEM):
    spectra, inputs, frame = filtered.shape
    columns = table.shape[0]
    height = columns // devices * ROWS
    assert first % height == 0
    split = 1
    while columns // split > 384 and devices % (2 * split) == 0:
        split *= 2
    in_specs = [
        pl.BlockSpec((columns // split, frame), lambda b, d: (d, 0)),
        pl.BlockSpec((ROWS, inputs, frame), lambda b, d: (b, 0, 0)),
    ]
    operands = [table, filtered]
    if buffer is not None:
        in_specs.append(pl.BlockSpec(memory_space=pl.ANY))
        operands.append(buffer)
    return pl.pallas_call(
        functools.partial(dft_kernel, inputs),
        grid=(spectra // ROWS, split),
        in_specs=in_specs,
        out_specs=pl.BlockSpec(
            (devices // split, height, inputs), lambda b, d: (d, first // height + b, 0)
        ),
        out_shape=jax.ShapeDtypeStruct((devices, rows, inputs), jnp.bfloat16),
        input_output_aliases={} if buffer is None else {2: 0},
        scratch_shapes=[pltpu.VMEM((columns // split * ROWS, inputs), jnp.float32)],
        compiler_params=pltpu.CompilerParams(vmem_limit_bytes=vmem),
        cost_estimate=pl.CostEstimate(
            flops=WEIGHT * columns * spectra * inputs * frame,
            bytes_accessed=2 * spectra * inputs * (frame + columns),
            transcendentals=0,
        ),
        name="dft",
    )(*operands)


def interleaved(block, fill, o_ref, right, left, across):
    depth, inputs = right.shape
    spectra = depth // 2

    def prepare(at):
        columns = pl.ds(at, block)
        fill(at, right)
        power = jnp.zeros((ROWS, block), jnp.float32)
        for row in range(0, depth, ROWS):
            piece = right[pl.ds(row, ROWS), columns].astype(jnp.float32)
            power = power + piece * piece
        scale = lax.rsqrt(jnp.sum(power, axis=0, keepdims=True) + 1e-06)
        across[:, columns] = jnp.broadcast_to(scale, (8, block))
        left[columns, :] = right[:, columns].T

    def multiply(at):
        rows, columns = pl.ds(at, block), pl.ds(0, at + block)
        own = left[rows, :]
        swapped = jnp.concatenate([own[:, spectra:], -own[:, :spectra]], axis=1)
        down = across[:, rows].T[:, :1]
        for part, operand in enumerate((own, swapped)):
            gram = jnp.dot(operand, right[:, columns], preferred_element_type=jnp.float32)
            scaled = (gram * down * across[:1, columns]).astype(jnp.bfloat16)
            o_ref[0, part, rows, columns] = scaled
            for before in range(0, at, block):
                mirror = scaled[:, before : before + block].T
                o_ref[0, part, pl.ds(before, block), rows] = -mirror if part else mirror

    prepare(0)
    for at in range(0, inputs, block):
        multiply(at)
        if at + block < inputs:
            prepare(at + block)


def correlate_kernel(block, slabs, blocks, *refs):
    sources, o_ref, scratch = refs[:blocks], refs[-4], refs[-3:]
    devices, _, width = sources[0].shape
    spectra = scratch[0].shape[0] // 2

    def fill(first, right):
        for part in range(2):
            for device in range(first // width * slabs, (first + block) // width * slabs):
                g, t = device // slabs, device % slabs
                for b, ref in enumerate(sources):
                    at = part * spectra + (t * blocks + b) * ROWS
                    right[pl.ds(at, ROWS), pl.ds(g * width, width)] = ref[
                        device, pl.ds(part * ROWS, ROWS), :
                    ]

    interleaved(block, fill, o_ref, *scratch)


def plain_correlate_kernel(block, r_ref, o_ref, *scratch):
    def fill(first, right):
        columns = pl.ds(first, block)
        right[:, columns] = r_ref[0, :, columns]

    interleaved(block, fill, o_ref, *scratch)


def correlate(kernel, in_specs, operands, total, first, count, out_shape, spectra):
    inputs = out_shape.shape[-1]
    aliases = {}
    if total is not None:
        aliases = {len(operands): 0}
        in_specs = [*in_specs, pl.BlockSpec(memory_space=pl.ANY)]
        operands = [*operands, total]
    scratch = [
        pltpu.VMEM((2 * spectra, inputs), jnp.bfloat16),
        pltpu.VMEM((inputs, 2 * spectra), jnp.bfloat16),
        pltpu.VMEM((8, inputs), jnp.float32),
    ]
    return pl.pallas_call(
        kernel,
        grid=(count,),
        in_specs=in_specs,
        out_specs=pl.BlockSpec((1, 2, inputs, inputs), lambda c: (first + c, 0, 0, 0)),
        out_shape=out_shape,
        input_output_aliases=aliases,
        scratch_shapes=scratch,
        compiler_params=pltpu.CompilerParams(vmem_limit_bytes=VMEM),
        cost_estimate=pl.CostEstimate(
            flops=8 * count * inputs * inputs * spectra,
            bytes_accessed=4 * count * inputs * (inputs + spectra),
            transcendentals=0,
        ),
        name="correlate",
    )(*operands)


def table_of(frame, devices, channels, first, count):
    channel = np.arange(devices)[:, None, None] * channels + first
    channel = channel + np.arange(count)[None, :, None]
    return dft_rows(frame, (2 * channel + np.arange(2)[None, None, :]).reshape(-1))


def exchange(rows):
    return lax.all_to_all(rows, ("inp", "tm"), split_axis=0, concat_axis=0, tiled=True)


def narrow(voltages, prototype, earlier, out_shape):
    inputs, samples = voltages.shape
    frame = prototype.shape[1]
    groups, slabs = lax.axis_size("inp"), lax.axis_size("tm")
    devices, channels = groups * slabs, out_shape.shape[0]
    spectra = samples // frame
    filtered = jnp.concatenate(
        [filter_edge(voltages, earlier, prototype), filter_main(voltages, prototype)]
    )
    table = table_of(frame, devices, channels, 0, channels)
    dims = (((1,), (2,)), ((), ()))
    rows = lax.dot_general(table, filtered, dims, preferred_element_type=jnp.float32)
    rows = rows.astype(jnp.bfloat16).reshape(devices, -1, inputs)
    turned = exchange(rows).reshape(groups, slabs, channels, 2, spectra, inputs)
    depth = 2 * slabs * spectra
    planes = turned.transpose(2, 3, 1, 4, 0, 5).reshape(channels, depth, groups * inputs)
    return correlate(
        functools.partial(plain_correlate_kernel, min(256, groups * inputs)),
        [pl.BlockSpec((1, depth, groups * inputs), lambda c: (c, 0, 0))],
        [planes],
        None,
        0,
        channels,
        out_shape,
        depth // 2,
    )


def shards(voltages, prototype):
    inputs, samples = voltages.shape
    taps, frame = prototype.shape
    spectra = samples // frame
    groups, slabs = lax.axis_size("inp"), lax.axis_size("tm")
    devices = groups * slabs
    channels = frame // 2 // devices
    total_inputs = groups * inputs
    out_shape = jax.ShapeDtypeStruct((channels, 2, total_inputs, total_inputs), jnp.bfloat16)
    earlier = shifted(voltages[:, (spectra - taps + 1) * frame :], "tm", 1)
    if inputs % LANES or channels % 16:
        return narrow(voltages, prototype, earlier, out_shape)

    middle = channels // 2
    last = channels // 8
    early = channels - middle - last
    blocks = spectra // ROWS
    unit = 2 * ROWS

    main = filter_main(voltages, prototype)
    rows = (blocks - 1) * early * unit
    table = table_of(frame, devices, channels, 0, early)
    first_turned = exchange(transform(table, main, devices, rows, 0, None, VMEM_FIRST))

    edge = filter_edge(voltages, earlier, prototype)
    rows = channels * unit + (blocks - 1) * middle * unit
    table = table_of(frame, devices, channels, 0, channels)
    buffer = transform(table, edge, devices, rows, 0, None)
    table = table_of(frame, devices, channels, early, middle)
    buffer = transform(table, main, devices, rows, channels * unit, buffer)
    middle_turned = exchange(buffer)

    rows = (blocks - 1) * last * unit
    table = table_of(frame, devices, channels, early + middle, last)
    last_turned = exchange(transform(table, main, devices, rows, 0, None))

    total = None
    first = 0
    for turned, count, base in (
        (first_turned, early, 0),
        (middle_turned, middle, channels),
        (last_turned, last, 0),
    ):
        bases = [first] + [base + b * count for b in range(blocks - 1)]
        in_specs = [
            pl.BlockSpec((devices, unit, inputs), lambda c, at=at: (0, at + c, 0))
            for at in bases
        ]
        operands = [middle_turned] + [turned] * (blocks - 1)
        kernel = functools.partial(correlate_kernel, min(256, total_inputs), slabs, blocks)
        total = correlate(
            kernel, in_specs, operands, total, first, count, out_shape, slabs * spectra
        )
        first += count
    return total


def solution(mesh):
    return jax.shard_map(
        shards,
        mesh=mesh,
        in_specs=(P("inp", "tm"), P()),
        out_specs=P(("inp", "tm"), None, None, None),
        check_vma=False,
    )
```

```python
import functools

import jax
import jax.numpy as jnp
import numpy as np
from jax import lax
from jax.experimental import pallas as pl
from jax.experimental.pallas import tpu as pltpu
from jax.sharding import PartitionSpec as P

LANES = 128
ROWS = 16
VMEM = 63 * 1024 * 1024
VMEM_FIRST = 56 * 1024 * 1024
WEIGHT = 8


def shifted(block, axis, distance):
    devices = range(lax.axis_size(axis))
    route = [(i - distance, i) for i in devices if i - distance in devices]
    return lax.ppermute(block, axis, route)


def dft_rows(frame, columns):
    sample = np.arange(frame, dtype=np.int64)[None, :]
    columns = columns[:, None]
    phase = (sample * (columns // 2) % frame) * (2.0 * np.pi / frame)
    table = np.where(columns % 2 == 0, np.cos(phase), -np.sin(phase))
    return jnp.asarray(table.astype(jnp.bfloat16))


def fir(load, store, coefficients, count):
    taps = len(coefficients)
    window = [load(f) for f in range(taps - 1)]
    for s in range(count):
        window.append(load(s + taps - 1))
        total = window[0] * coefficients[0]
        for k in range(1, taps):
            total = total + window[k] * coefficients[k]
        store(s, total)
        window.pop(0)


def main_filter_kernel(taps, frame, spectra, skip, v_ref, p_ref, o_ref):
    @pl.loop(0, frame // LANES)
    def _(block):
        at = pl.multiple_of(block * LANES, LANES)
        lanes = pl.ds(at, LANES)
        coefficients = [
            jnp.broadcast_to(p_ref[pl.ds(k, 1), lanes], (ROWS, LANES)) for k in range(taps)
        ]
        first = skip - taps + 1

        def load(f):
            return v_ref[:, pl.ds((first + f) * frame + at, LANES)].astype(jnp.float32)

        def store(s, value):
            o_ref[s, :, lanes] = value.astype(jnp.bfloat16)

        fir(load, store, coefficients, spectra - skip)


def edge_filter_kernel(taps, frame, skip, v_ref, e_ref, p_ref, o_ref):
    @pl.loop(0, frame // LANES)
    def _(block):
        at = pl.multiple_of(block * LANES, LANES)
        lanes = pl.ds(at, LANES)
        coefficients = [
            jnp.broadcast_to(p_ref[pl.ds(k, 1), lanes], (ROWS, LANES)) for k in range(taps)
        ]

        def load(f):
            if f < taps - 1:
                return e_ref[:, pl.ds(f * frame + at, LANES)].astype(jnp.float32)
            return v_ref[:, pl.ds((f - taps + 1) * frame + at, LANES)].astype(jnp.float32)

        def store(s, value):
            o_ref[s, :, lanes] = value.astype(jnp.bfloat16)

        fir(load, store, coefficients, skip)


def filter_main(voltages, prototype):
    inputs, samples = voltages.shape
    taps, frame = prototype.shape
    spectra = samples // frame
    assert taps - 1 <= ROWS < spectra
    return pl.pallas_call(
        functools.partial(main_filter_kernel, taps, frame, spectra, ROWS),
        grid=(inputs // ROWS,),
        in_specs=[
            pl.BlockSpec((ROWS, samples), lambda r: (r, 0)),
            pl.BlockSpec((taps, frame), lambda r: (0, 0)),
        ],
        out_specs=pl.BlockSpec((spectra - ROWS, ROWS, frame), lambda r: (0, r, 0)),
        out_shape=jax.ShapeDtypeStruct((spectra - ROWS, inputs, frame), jnp.bfloat16),
        compiler_params=pltpu.CompilerParams(vmem_limit_bytes=VMEM_FIRST),
        cost_estimate=pl.CostEstimate(
            flops=2 * taps * inputs * samples,
            bytes_accessed=4 * inputs * samples,
            transcendentals=0,
        ),
        name="filter_main",
    )(voltages, prototype)


def filter_edge(voltages, earlier, prototype):
    inputs = voltages.shape[0]
    taps, frame = prototype.shape
    return pl.pallas_call(
        functools.partial(edge_filter_kernel, taps, frame, ROWS),
        grid=(inputs // ROWS,),
        in_specs=[
            pl.BlockSpec((ROWS, ROWS * frame), lambda r: (r, 0)),
            pl.BlockSpec((ROWS, (taps - 1) * frame), lambda r: (r, 0)),
            pl.BlockSpec((taps, frame), lambda r: (0, 0)),
        ],
        out_specs=pl.BlockSpec((ROWS, ROWS, frame), lambda r: (0, r, 0)),
        out_shape=jax.ShapeDtypeStruct((ROWS, inputs, frame), jnp.bfloat16),
        compiler_params=pltpu.CompilerParams(vmem_limit_bytes=VMEM),
        cost_estimate=pl.CostEstimate(
            flops=512 * WEIGHT * taps * inputs * ROWS * frame,
            bytes_accessed=6 * inputs * ROWS * frame,
            transcendentals=0,
        ),
        name="filter_edge",
    )(voltages, earlier, prototype)


def dft_kernel(inputs, t_ref, f_ref, *refs):
    o_ref, turn = refs[-2], refs[-1]
    columns = t_ref.shape[0]
    group = max(1, 256 // inputs)
    for s in range(0, ROWS, group):
        frames = f_ref[pl.ds(s, group)].reshape(group * inputs, f_ref.shape[2])
        product = lax.dot_general(
            t_ref[...], frames, (((1,), (1,)), ((), ())), preferred_element_type=jnp.float32
        )
        for part in range(group):
            turn[pl.ds(s + part, columns, stride=ROWS), :] = product[
                :, part * inputs : (part + 1) * inputs
            ]
    o_ref[...] = turn[...].reshape(o_ref.shape).astype(jnp.bfloat16)


def transform(table, filtered, devices, rows, first, buffer, vmem=VMEM):
    spectra, inputs, frame = filtered.shape
    columns = table.shape[0]
    height = columns // devices * ROWS
    assert first % height == 0
    split = 1
    while columns // split > 384 and devices % (2 * split) == 0:
        split *= 2
    in_specs = [
        pl.BlockSpec((columns // split, frame), lambda b, d: (d, 0)),
        pl.BlockSpec((ROWS, inputs, frame), lambda b, d: (b, 0, 0)),
    ]
    operands = [table, filtered]
    if buffer is not None:
        in_specs.append(pl.BlockSpec(memory_space=pl.ANY))
        operands.append(buffer)
    return pl.pallas_call(
        functools.partial(dft_kernel, inputs),
        grid=(spectra // ROWS, split),
        in_specs=in_specs,
        out_specs=pl.BlockSpec(
            (devices // split, height, inputs), lambda b, d: (d, first // height + b, 0)
        ),
        out_shape=jax.ShapeDtypeStruct((devices, rows, inputs), jnp.bfloat16),
        input_output_aliases={} if buffer is None else {2: 0},
        scratch_shapes=[pltpu.VMEM((columns // split * ROWS, inputs), jnp.float32)],
        compiler_params=pltpu.CompilerParams(vmem_limit_bytes=vmem),
        cost_estimate=pl.CostEstimate(
            flops=WEIGHT * columns * spectra * inputs * frame,
            bytes_accessed=2 * spectra * inputs * (frame + columns),
            transcendentals=0,
        ),
        name="dft",
    )(*operands)


def interleaved(block, fill, o_ref, right, left, across):
    depth, inputs = right.shape
    spectra = depth // 2

    def prepare(at):
        columns = pl.ds(at, block)
        fill(at, right)
        power = jnp.zeros((ROWS, block), jnp.float32)
        for row in range(0, depth, ROWS):
            piece = right[pl.ds(row, ROWS), columns].astype(jnp.float32)
            power = power + piece * piece
        scale = lax.rsqrt(jnp.sum(power, axis=0, keepdims=True) + 1e-06)
        across[:, columns] = jnp.broadcast_to(scale, (8, block))
        left[columns, :] = right[:, columns].T

    def multiply(at, part):
        rows, columns = pl.ds(at, block), pl.ds(0, at + block)
        operand = left[rows, :]
        if part:
            operand = jnp.concatenate([operand[:, spectra:], -operand[:, :spectra]], axis=1)
        down = across[:, rows].T[:, :1]
        gram = jnp.dot(operand, right[:, columns], preferred_element_type=jnp.float32)
        scaled = (gram * down * across[:1, columns]).astype(jnp.bfloat16)
        o_ref[0, 0, rows, columns] = scaled
        for before in range(0, at, block):
            mirror = scaled[:, before : before + block].T
            o_ref[0, 0, pl.ds(before, block), rows] = -mirror if part else mirror

    @pl.when(pl.program_id(1) == 0)
    def _():
        prepare(0)
        for at in range(0, inputs, block):
            multiply(at, 0)
            if at + block < inputs:
                prepare(at + block)

    @pl.when(pl.program_id(1) == 1)
    def _():
        for at in range(0, inputs, block):
            multiply(at, 1)


def correlate_kernel(block, slabs, blocks, *refs):
    sources, o_ref, scratch = refs[:blocks], refs[-4], refs[-3:]
    devices, _, width = sources[0].shape
    spectra = scratch[0].shape[0] // 2

    def fill(first, right):
        for part in range(2):
            for device in range(first // width * slabs, (first + block) // width * slabs):
                g, t = device // slabs, device % slabs
                for b, ref in enumerate(sources):
                    at = part * spectra + (t * blocks + b) * ROWS
                    right[pl.ds(at, ROWS), pl.ds(g * width, width)] = ref[
                        device, pl.ds(part * ROWS, ROWS), :
                    ]

    interleaved(block, fill, o_ref, *scratch)


def plain_correlate_kernel(block, r_ref, o_ref, *scratch):
    def fill(first, right):
        columns = pl.ds(first, block)
        right[:, columns] = r_ref[0, :, columns]

    interleaved(block, fill, o_ref, *scratch)


def correlate(kernel, in_specs, operands, total, first, count, out_shape, spectra):
    inputs = out_shape.shape[-1]
    aliases = {}
    if total is not None:
        aliases = {len(operands): 0}
        in_specs = [*in_specs, pl.BlockSpec(memory_space=pl.ANY)]
        operands = [*operands, total]
    scratch = [
        pltpu.VMEM((2 * spectra, inputs), jnp.bfloat16),
        pltpu.VMEM((inputs, 2 * spectra), jnp.bfloat16),
        pltpu.VMEM((8, inputs), jnp.float32),
    ]
    return pl.pallas_call(
        kernel,
        grid=(count, 2),
        in_specs=in_specs,
        out_specs=pl.BlockSpec((1, 1, inputs, inputs), lambda c, part: (first + c, part, 0, 0)),
        out_shape=out_shape,
        input_output_aliases=aliases,
        scratch_shapes=scratch,
        compiler_params=pltpu.CompilerParams(vmem_limit_bytes=VMEM),
        cost_estimate=pl.CostEstimate(
            flops=8 * count * inputs * inputs * spectra,
            bytes_accessed=4 * count * inputs * (inputs + spectra),
            transcendentals=0,
        ),
        name="correlate",
    )(*operands)


def table_of(frame, devices, channels, first, count):
    channel = np.arange(devices)[:, None, None] * channels + first
    channel = channel + np.arange(count)[None, :, None]
    return dft_rows(frame, (2 * channel + np.arange(2)[None, None, :]).reshape(-1))


def exchange(rows):
    return lax.all_to_all(rows, ("inp", "tm"), split_axis=0, concat_axis=0, tiled=True)


def narrow(voltages, prototype, earlier, out_shape):
    inputs, samples = voltages.shape
    frame = prototype.shape[1]
    groups, slabs = lax.axis_size("inp"), lax.axis_size("tm")
    devices, channels = groups * slabs, out_shape.shape[0]
    spectra = samples // frame
    filtered = jnp.concatenate(
        [filter_edge(voltages, earlier, prototype), filter_main(voltages, prototype)]
    )
    table = table_of(frame, devices, channels, 0, channels)
    dims = (((1,), (2,)), ((), ()))
    rows = lax.dot_general(table, filtered, dims, preferred_element_type=jnp.float32)
    rows = rows.astype(jnp.bfloat16).reshape(devices, -1, inputs)
    turned = exchange(rows).reshape(groups, slabs, channels, 2, spectra, inputs)
    depth = 2 * slabs * spectra
    planes = turned.transpose(2, 3, 1, 4, 0, 5).reshape(channels, depth, groups * inputs)
    return correlate(
        functools.partial(plain_correlate_kernel, min(256, groups * inputs)),
        [pl.BlockSpec((1, depth, groups * inputs), lambda c, part: (c, 0, 0))],
        [planes],
        None,
        0,
        channels,
        out_shape,
        depth // 2,
    )


def shards(voltages, prototype):
    inputs, samples = voltages.shape
    taps, frame = prototype.shape
    spectra = samples // frame
    groups, slabs = lax.axis_size("inp"), lax.axis_size("tm")
    devices = groups * slabs
    channels = frame // 2 // devices
    total_inputs = groups * inputs
    out_shape = jax.ShapeDtypeStruct((channels, 2, total_inputs, total_inputs), jnp.bfloat16)
    earlier = shifted(voltages[:, (spectra - taps + 1) * frame :], "tm", 1)
    if inputs % LANES or channels % 16:
        return narrow(voltages, prototype, earlier, out_shape)

    middle = channels // 2
    last = channels // 8
    early = channels - middle - last
    blocks = spectra // ROWS
    unit = 2 * ROWS

    main = filter_main(voltages, prototype)
    rows = (blocks - 1) * early * unit
    table = table_of(frame, devices, channels, 0, early)
    first_turned = exchange(transform(table, main, devices, rows, 0, None, VMEM_FIRST))

    edge = filter_edge(voltages, earlier, prototype)
    rows = channels * unit + (blocks - 1) * middle * unit
    table = table_of(frame, devices, channels, 0, channels)
    buffer = transform(table, edge, devices, rows, 0, None)
    table = table_of(frame, devices, channels, early, middle)
    buffer = transform(table, main, devices, rows, channels * unit, buffer)
    middle_turned = exchange(buffer)

    rows = (blocks - 1) * last * unit
    table = table_of(frame, devices, channels, early + middle, last)
    last_turned = exchange(transform(table, main, devices, rows, 0, None))

    total = None
    first = 0
    for turned, count, base in (
        (first_turned, early, 0),
        (middle_turned, middle, channels),
        (last_turned, last, 0),
    ):
        bases = [first] + [base + b * count for b in range(blocks - 1)]
        in_specs = [
            pl.BlockSpec((devices, unit, inputs), lambda c, part, at=at: (0, at + c, 0))
            for at in bases
        ]
        operands = [middle_turned] + [turned] * (blocks - 1)
        kernel = functools.partial(correlate_kernel, min(256, total_inputs), slabs, blocks)
        total = correlate(
            kernel, in_specs, operands, total, first, count, out_shape, slabs * spectra
        )
        first += count
    return total


def solution(mesh):
    return jax.shard_map(
        shards,
        mesh=mesh,
        in_specs=(P("inp", "tm"), P()),
        out_specs=P(("inp", "tm"), None, None, None),
        check_vma=False,
    )
```
